256 devices in a mesh: feed: 64 (over y, x, z_hi, core), band: 4 (over z_lo).
Axes of the slice: x: 4, y: 4, z: 8 (z_hi: 2, z_lo: 4; z = z_hi * 4 + z_lo), core: 2. Of those that a mesh axis runs over, the one named last changes fastest.
Arguments:
- voltages: bfloat16 [2, 2048, 114688], P(None, ('band', 'feed')), may hold values from -6 to 6
- filter_taps: float32 [4, 16384], replicated, may hold values from -1 to 1
- feed_gains: bfloat16 [2, 64, 2048, 256], P(None, 'feed', 'band'), may hold values from 0.5 to 1.5
- beam_weights: bfloat16 [2, 64, 1024, 2048], P(None, 'feed', None, 'band'), may hold values from -0.125 to 0.125
- beam_mask: int32 [1024, 64], replicated, may hold values 0 or 1
- band_order: int32 [64], replicated, may hold values from 0 to 63, each once
Outputs:
- visibility: bfloat16 [2, 64, 2048, 2048], P(None, 'feed', 'band')
- beam_out: bfloat16 [64, 1024, 2, 4, 256], P('feed', 'band')
The draws below stay inside these ranges and needn't reach their ends.
Inputs may be any that keep to these rules, and one draw needn't show every extreme that they name: `band_order`: each of the 64 channel blocks goes to exactly one slot.
All inputs are finite; a program needn't handle non-finite values.
Results may differ from the reference program's by a relative error of at most 0.015.
Values may be sent and summed in bfloat16 or wider, within the bound.
No kernel may reach another device: no remote copies, remote signals or barrier semaphores. Data moves between devices by JAX's collectives and lax.ppermute only.
A program may use at most 128 MiB of HBM per device.

```python
import math
from functools import partial
import jax
import jax.numpy as jnp
from jax import lax

FEEDS = 2048
BEAMS = 1024
RADIX = 128
TAPS = 4
TILE = 32
SPECTRA = 4
CH = 16384
NBLK = 64
CHB = 256
TILES = 64
TIME = 114688


def set_ends(entries, stream_key, low, top_value):
    longest = entries.shape.index(max(entries.shape))
    spots = []
    for shift in (0, 1):
        where = [jax.random.randint(jax.random.fold_in(stream_key, axis), (), 0, length) for axis, length in enumerate(entries.shape)]
        where[longest] = (where[longest] + shift) % entries.shape[longest]
        spots.append(tuple(where))
    return entries.at[spots[0]].set(low).at[spots[1]].set(top_value)


def steps_of(key, shape, shards, least, largest):
    def one(axis_at, blocks):
        heights = jax.random.uniform(jax.random.fold_in(jax.random.fold_in(key, 6), axis_at), (blocks,), jnp.float32, least / len(shards), largest / len(shards))
        return jnp.repeat(jnp.exp(heights), shape[axis_at] // blocks).reshape((-1,) + (1,) * (len(shape) - axis_at - 1))

    level = one(*shards[0])
    for cut in shards[1:]:
        level = level * one(*cut)
    return level


def centred(stream_key, dims, scale, bound, cuts=(), kind=jnp.bfloat16):
    loudness = steps_of(stream_key, dims, cuts, -0.22, 0.18) if cuts else 1.0
    values = jax.random.normal(stream_key, dims, jnp.float32) * scale * loudness
    return jnp.minimum(jnp.maximum(values, -bound), bound).astype(kind)


def setup_inputs(seed: int = 0) -> dict:
    key_list = jax.random.split(jax.random.key(seed), 7)
    voltages = centred(key_list[0], (2, FEEDS, TIME), 1.0, 6.0, ((1, 256),))
    filter_taps = jnp.clip(jax.random.uniform(key_list[1], (TAPS, CH), jnp.float32, -1.0, 1.0), -1.0, 1.0)
    feed_gains = jnp.clip(1.0 + 0.1 * jax.random.normal(key_list[2], (2, NBLK, FEEDS, CHB), jnp.float32), 0.5, 1.5).astype(jnp.bfloat16)
    beam_weights = centred(key_list[3], (2, NBLK, BEAMS, FEEDS), FEEDS ** -0.5, 0.125, ((1, 64), (3, 4)))
    beam_mask = set_ends((jax.random.randint(key_list[4], (BEAMS, TILES), 0, 4) < 3).astype(jnp.int32), jax.random.fold_in(key_list[4], 1), 0, 1)
    band_order = jax.random.permutation(key_list[5], NBLK).astype(jnp.int32)
    return {"voltages": voltages, "filter_taps": filter_taps, "feed_gains": feed_gains, "beam_weights": beam_weights, "beam_mask": beam_mask, "band_order": band_order}


def dft_tables(radix, length):
    index_row = jnp.arange(radix, dtype=jnp.int32)
    product = index_row[:, None] * index_row[None, :] % radix
    angles = product.astype(jnp.float32) * (2.0 * math.pi / radix)
    factor = 1.0 / math.sqrt(radix)
    table_re = (jnp.cos(angles) * factor).astype(jnp.bfloat16)
    table_im = (-jnp.sin(angles) * factor).astype(jnp.bfloat16)
    twiddle = (index_row[:, None] * index_row[None, :] % length).astype(jnp.float32) * (2.0 * math.pi / length)
    return (table_re, table_im, jnp.cos(twiddle), -jnp.sin(twiddle))

def filter_frames(voltages, filter_taps):
    tap_count, length = filter_taps.shape
    frames = voltages.shape[2] // length
    spectra_count = frames - tap_count + 1
    framed = voltages.reshape(2, voltages.shape[1], frames, length)
    summed = filter_taps[0] * framed[:, :, 0:spectra_count].astype(jnp.float32)
    for tap_index in range(1, tap_count):
        summed = summed + filter_taps[tap_index] * framed[:, :, tap_index:tap_index + spectra_count].astype(jnp.float32)
    return summed.astype(jnp.bfloat16)

def section_first(dft_table, values_in):
    return jnp.einsum('kn,...nm->...km', dft_table, values_in)

def section_second(dft_table, values_in):
    return jnp.einsum('jm,...km->...jk', dft_table, values_in)

def channelize(voltages, filter_taps, radix):
    filtered = filter_frames(voltages, filter_taps)
    length = filter_taps.shape[1]
    feed_count = filtered.shape[1]
    spectra_count = filtered.shape[2]
    split_frame = filtered.reshape(2, feed_count, spectra_count, radix, radix).astype(jnp.float32)
    table_re, table_im, twid_re, twid_im = dft_tables(radix, length)
    table_re = table_re.astype(jnp.float32)
    table_im = table_im.astype(jnp.float32)
    first_re = section_first(table_re, split_frame[0]) - section_first(table_im, split_frame[1])
    first_im = section_first(table_re, split_frame[1]) + section_first(table_im, split_frame[0])
    rotated = jnp.stack([first_re * twid_re - first_im * twid_im, first_re * twid_im + first_im * twid_re])
    rotated = lax.optimization_barrier(rotated.astype(jnp.bfloat16)).astype(jnp.float32)
    out_re = section_second(table_re, rotated[0]) - section_second(table_im, rotated[1])
    out_im = section_second(table_re, rotated[1]) + section_second(table_im, rotated[0])
    return jnp.stack([out_re, out_im]).astype(jnp.bfloat16).reshape(2, feed_count, spectra_count, length)

def slot_outputs(spectra, feed_gains, beam_weights, mask_full, band_order, slot_index):
    block_width = feed_gains.shape[3]
    feed_count = spectra.shape[1]
    spectra_count = spectra.shape[2]
    offset = band_order[slot_index].astype(jnp.int32) * block_width
    channel_part = lax.dynamic_slice_in_dim(spectra, offset, block_width, 3).astype(jnp.float32)
    gain_block = lax.dynamic_index_in_dim(feed_gains, slot_index, 1, keepdims=False).astype(jnp.float32)[:, :, None, :]
    calib_re = gain_block[0] * channel_part[0] - gain_block[1] * channel_part[1]
    calib_im = gain_block[0] * channel_part[1] + gain_block[1] * channel_part[0]
    rounded = lax.optimization_barrier(jnp.stack([calib_re, calib_im]).astype(jnp.bfloat16)).astype(jnp.float32)
    flattened = rounded.reshape(2, feed_count, spectra_count * block_width)
    average = 1.0 / (spectra_count * block_width)
    vis_re = jnp.dot(flattened[0], flattened[0].T, preferred_element_type=jnp.float32) + jnp.dot(flattened[1], flattened[1].T, preferred_element_type=jnp.float32)
    vis_im = jnp.dot(flattened[1], flattened[0].T, preferred_element_type=jnp.float32) - jnp.dot(flattened[0], flattened[1].T, preferred_element_type=jnp.float32)
    visibility = (jnp.stack([vis_re, vis_im]) * average).astype(jnp.bfloat16)
    weights = lax.dynamic_index_in_dim(beam_weights, slot_index, 1, keepdims=False).astype(jnp.float32) * mask_full
    beam_re = jnp.dot(weights[0], flattened[0], preferred_element_type=jnp.float32) - jnp.dot(weights[1], flattened[1], preferred_element_type=jnp.float32)
    beam_im = jnp.dot(weights[0], flattened[1], preferred_element_type=jnp.float32) + jnp.dot(weights[1], flattened[0], preferred_element_type=jnp.float32)
    beam_count = weights.shape[1]
    beam_out = jnp.stack([beam_re, beam_im], axis=1).reshape(beam_count, 2, spectra_count, block_width).astype(jnp.bfloat16)
    return (visibility, beam_out)

def reference(voltages, filter_taps, feed_gains, beam_weights, beam_mask, band_order):
    group_size = 64
    groups = FEEDS // group_size

    def one_group(group_index):
        piece_volts = lax.dynamic_slice_in_dim(voltages, group_index * group_size, group_size, 1)
        return channelize(piece_volts, filter_taps, RADIX)
    group_spectra = lax.map(one_group, jnp.arange(groups, dtype=jnp.int32))
    spectra = jnp.moveaxis(group_spectra, 0, 1).reshape(2, FEEDS, SPECTRA, CH)
    mask_full = jnp.repeat(beam_mask, TILE, axis=1).astype(jnp.float32)
    worker = partial(slot_outputs, spectra, feed_gains, beam_weights, mask_full, band_order)
    visibility, beam_out = lax.map(worker, jnp.arange(NBLK, dtype=jnp.int32))
    return (jnp.moveaxis(visibility, 0, 1), beam_out)
```

```python
import math

import jax
import jax.numpy as jnp
import numpy as np
from jax import lax
from jax.experimental import pallas as pl
from jax.experimental.pallas import tpu as pltpu
from jax.sharding import PartitionSpec as P

RADIX = 128
TILE = 32
SIDE = 4
BOTH = ("feed", "band")
F32 = jnp.float32
BF16 = jnp.bfloat16


def feed_at(y, x, half, core):
    return ((y * SIDE + x) * 2 + half) * 2 + core


PLANE_GROUPS = [
    [feed_at(y, x, half, core) for y in range(SIDE) for x in range(SIDE) for core in range(2)]
    for half in range(2)
]


def hop(step, senders):
    pairs = []
    for y in range(SIDE):
        for x in range(SIDE):
            for core in range(2):
                for z in range(8):
                    if z % 4 in senders:
                        to = (z + step) % 8
                        pairs.append(
                            (feed_at(y, x, z // 4, core) * 4 + z % 4, feed_at(y, x, to // 4, core) * 4 + to % 4)
                        )
    return pairs


def constants(length):
    row = np.arange(RADIX)
    angles = (row[:, None] * row[None, :] % RADIX) * (2.0 * math.pi / RADIX)
    factor = 1.0 / math.sqrt(RADIX)
    re = (np.cos(angles) * factor).astype(np.float32)
    im = (-np.sin(angles) * factor).astype(np.float32)
    first = np.block([[re, -im], [im, re]])
    second = np.stack([np.hstack([re, -im]), np.hstack([im, re])])
    second = second.reshape(2, RADIX // 2, 2, 2 * RADIX).transpose(0, 2, 1, 3).reshape(4, RADIX // 2, 2 * RADIX)
    twiddle = (row[:, None] * row[None, :] % length) * (2.0 * math.pi / length)
    tw = np.stack([np.cos(twiddle), -np.sin(twiddle)]).astype(np.float32)
    place = np.zeros((64, 64), np.float32)
    for yx in range(16):
        for core in range(2):
            for half in range(2):
                place[(yx * 2 + core) * 2 + half, (yx * 2 + half) * 2 + core] = 1.0
    return (jnp.asarray(first, BF16), jnp.asarray(second, BF16), jnp.asarray(tw), jnp.asarray(place, BF16))


def channel_kernel(start, order_ref, place_ref, first_ref, second_ref, tw_ref, taps_ref, volts_ref, out_ref, frame, turned, lhs):
    length = taps_ref.shape[1]
    pick = (order_ref[...] == lax.broadcasted_iota(jnp.int32, (64, 64), 1)).astype(BF16)
    pick = jnp.dot(place_ref[...], pick, preferred_element_type=F32).astype(BF16)
    for part in range(4):
        lhs[part * 64 : (part + 1) * 64, :] = jnp.dot(pick, second_ref[part], preferred_element_type=F32).astype(BF16)

    width = 16 * RADIX

    def filter_chunk(chunk, carry):
        lane = pl.multiple_of(chunk * width, width)
        taps = [jnp.broadcast_to(taps_ref[t : t + 1, pl.ds(lane, width)], (8, width)) for t in range(4)]
        for part in range(2):
            volts = [
                volts_ref[part, :, pl.ds((start + n) * length + lane, width)].astype(F32) for n in range(5)
            ]
            for s in range(2):
                total = taps[0] * volts[s]
                for t in range(1, 4):
                    total = total + taps[t] * volts[s + t]
                for a in range(16):
                    at = pl.multiple_of(chunk * width // RADIX * 8 + a * 8, 8)
                    frame[s, part, pl.ds(at, 8), :] = total[:, a * RADIX : (a + 1) * RADIX]
        return carry

    lax.fori_loop(0, length // width, filter_chunk, 0)
    tw_re, tw_im = tw_ref[0], tw_ref[1]
    for f in range(8):
        columns = []
        for s in range(2):
            parts = [frame[s, part, pl.ds(f, RADIX, stride=8), :] for part in range(2)]
            columns.append(jnp.concatenate(parts, axis=0))
        values = jnp.concatenate(columns, axis=1).astype(BF16)
        mid = jnp.dot(first_ref[...], values, preferred_element_type=F32)
        rows = []
        for s in range(2):
            re = mid[:RADIX, s * RADIX : (s + 1) * RADIX]
            im = mid[RADIX:, s * RADIX : (s + 1) * RADIX]
            rows.append(jnp.concatenate([re * tw_re - im * tw_im, re * tw_im + im * tw_re], axis=1).astype(BF16))
        rotated = jnp.concatenate(rows, axis=0)
        out = lax.dot_general(lhs[...], rotated, (((1,), (1,)), ((), ())), preferred_element_type=F32)
        for part in range(2):
            for h in range(2):
                for s in range(2):
                    at = part * RADIX + h * 64
                    turned[part * 4 + s * 2 + h, pl.ds(f, 64, stride=8), :] = out[at : at + 64, s * RADIX : (s + 1) * RADIX]
    for block in range(8):
        out_ref[:, :, block * RADIX : (block + 1) * RADIX] = turned[block].reshape(32, 16, RADIX).astype(BF16)


def channelize(start, voltages, filter_taps, band_order):
    first, second, tw, place = constants(filter_taps.shape[1])
    vmem = pl.BlockSpec(memory_space=pltpu.VMEM)
    return pl.pallas_call(
        lambda *refs: channel_kernel(start, *refs),
        out_shape=jax.ShapeDtypeStruct((32, 16, 1024), BF16),
        in_specs=[vmem] * 7,
        out_specs=vmem,
        scratch_shapes=[
            pltpu.VMEM((2, 2, 8 * RADIX, RADIX), F32),
            pltpu.VMEM((8, 512, RADIX), F32),
            pltpu.VMEM((256, 256), BF16),
        ],
        compiler_params=pltpu.CompilerParams(vmem_limit_bytes=48 * 2**20),
        name="channelize",
    )(band_order.reshape(64, 1), place, first, second, tw, filter_taps, voltages)


def calibrate_kernel(at_ref, got_ref, own_gain_ref, other_gain_ref, own_ref, other_ref):
    half = at_ref[0]
    got = got_ref[...].astype(F32)
    low, high = got[:, :8], got[:, 8:]
    gains = (own_gain_ref[:, :, half], other_gain_ref[...])
    for which, (gain, out_ref) in enumerate(zip(gains, (own_ref, other_ref))):
        take_low = half == which
        gain = gain.astype(F32).reshape(2, 32, 8, 256)
        for s in range(2):
            re_at, im_at = slice(s * 256, (s + 1) * 256), slice(512 + s * 256, 512 + (s + 1) * 256)
            re = jnp.where(take_low, low[:, :, re_at], high[:, :, re_at])
            im = jnp.where(take_low, low[:, :, im_at], high[:, :, im_at])
            out_ref[:, re_at] = (gain[0] * re - gain[1] * im).reshape(256, 256).astype(BF16)
            out_ref[:, im_at] = (gain[0] * im + gain[1] * re).reshape(256, 256).astype(BF16)


def calibrate(half, got, own_gain, other_gain):
    vmem = pl.BlockSpec(memory_space=pltpu.VMEM)
    return pl.pallas_call(
        calibrate_kernel,
        out_shape=[jax.ShapeDtypeStruct((256, 1024), BF16)] * 2,
        in_specs=[pl.BlockSpec(memory_space=pltpu.SMEM)] + [vmem] * 3,
        out_specs=[vmem] * 2,
        compiler_params=pltpu.CompilerParams(vmem_limit_bytes=48 * 2**20),
        name="calibrate",
    )(half.reshape(1), got, own_gain, other_gain)


def weights_kernel(at_ref, mask_ref, own_ref, near_ref, far_ref, end_ref, out_ref):
    band = at_ref[0]
    low = band < 2
    outer = jnp.where(low, 0, 3)
    near_group = jnp.where(low, 2, 1)
    far_group = jnp.where(low, 3, 0)
    end_group = jnp.where(low, 1 - band, 5 - band)
    own_row = pl.multiple_of(jnp.where(low, 256, 0), 256)
    outer_row = pl.multiple_of(jnp.where(low, 0, 256), 256)
    masks = []
    for rows in (band, outer):
        cols = mask_ref[pl.ds(pl.multiple_of(rows * 256, 256), 256), :].astype(F32).astype(BF16)
        masks.append(cols)

    def spread(which, group):
        tile = lax.broadcasted_iota(jnp.int32, (64, 512), 0)
        column = lax.broadcasted_iota(jnp.int32, (64, 512), 1) // TILE + group * 16
        return jnp.dot(masks[which], (tile == column).astype(BF16), preferred_element_type=F32).astype(BF16)

    for group, src_ref, rows in (
        (band, own_ref, (band * 256, outer * 256)),
        (near_group, near_ref, (own_row, outer_row)),
        (far_group, far_ref, (own_row, outer_row)),
        (end_group, end_ref, (0, None)),
    ):
        lanes = pl.ds(pl.multiple_of(group * 512, 512), 512)
        for which, row in enumerate(rows):
            for part in range(2):
                at = slice((which * 2 + part) * 256, (which * 2 + part + 1) * 256)
                if row is None:
                    out_ref[at, lanes] = jnp.zeros((256, 512), BF16)
                else:
                    taken = src_ref[part, pl.ds(pl.multiple_of(row, 256), 256), :]
                    out_ref[at, lanes] = taken * spread(which, group)


def weight_rows(band, mask, own, near, far, end):
    vmem = pl.BlockSpec(memory_space=pltpu.VMEM)
    return pl.pallas_call(
        weights_kernel,
        out_shape=jax.ShapeDtypeStruct((1024, 2048), BF16),
        in_specs=[pl.BlockSpec(memory_space=pltpu.SMEM)] + [vmem] * 5,
        out_specs=vmem,
        compiler_params=pltpu.CompilerParams(vmem_limit_bytes=48 * 2**20),
        name="weight_rows",
    )(band.reshape(1), mask, own, near, far, end)


def pair_kernel(average, at_ref, left_a, left_b, right_a, right_b, out_ref):
    re = im = None
    for left_ref, right_ref in ((left_a, right_a), (left_b, right_b)):
        left, right = left_ref[...], right_ref[...]
        half = left.shape[1] // 2
        crossed = jnp.concatenate([left[:, half:], -left[:, :half]], axis=1)
        dims = (((1,), (1,)), ((), ()))
        now_re = lax.dot_general(left, right, dims, preferred_element_type=F32)
        now_im = lax.dot_general(crossed, right, dims, preferred_element_type=F32)
        re = now_re if re is None else re + now_re
        im = now_im if im is None else im + now_im
    out_ref[0] = (re * average).astype(BF16)
    out_ref[1] = (im * average).astype(BF16)


def pairs(average, row_block, first_col, blocks, width, sections):
    rows, depth = 512, sections[0].shape[1]
    left = pl.BlockSpec((rows, depth), lambda i, at: (at[0], 0))
    right = pl.BlockSpec((width, depth), lambda i, at: (at[1] + i, 0))
    return pl.pallas_call(
        lambda *refs: pair_kernel(average, *refs),
        out_shape=jax.ShapeDtypeStruct((2, rows, blocks * width), BF16),
        grid_spec=pltpu.PrefetchScalarGridSpec(
            num_scalar_prefetch=1,
            grid=(blocks,),
            in_specs=[left, left, right, right],
            out_specs=pl.BlockSpec((2, rows, width), lambda i, at: (0, 0, i)),
        ),
        compiler_params=pltpu.CompilerParams(vmem_limit_bytes=48 * 2**20),
        cost_estimate=pl.CostEstimate(
            flops=8 * rows * blocks * width * depth, bytes_accessed=4 * depth * (rows + blocks * width), transcendentals=0
        ),
        name="pairs",
    )(jnp.stack([row_block, first_col]), sections[0], sections[1], sections[0], sections[1])


def beam_kernel(weight_ref, section_ref, out_ref):
    half = section_ref.shape[1] // 2
    total = jnp.dot(weight_ref[...], section_ref[...], preferred_element_type=F32)
    out_ref[:, :half] = (total[:256, :half] - total[256:, half:]).astype(out_ref.dtype)
    out_ref[:, half:] = (total[:256, half:] + total[256:, :half]).astype(out_ref.dtype)


def beams(which, weights, section, dtype):
    feeds, depth = section.shape
    return pl.pallas_call(
        beam_kernel,
        out_shape=jax.ShapeDtypeStruct((256, depth), dtype),
        grid=(1,),
        in_specs=[pl.BlockSpec((512, feeds), lambda i: (which, 0)), pl.BlockSpec((feeds, depth), lambda i: (0, 0))],
        out_specs=pl.BlockSpec((256, depth), lambda i: (0, 0)),
        compiler_params=pltpu.CompilerParams(vmem_limit_bytes=48 * 2**20),
        cost_estimate=pl.CostEstimate(
            flops=4 * 256 * feeds * depth, bytes_accessed=2 * feeds * (depth + 512), transcendentals=0
        ),
        name="beams",
    )(weights, section)


def shards(voltages, filter_taps, feed_gains, beam_weights, beam_mask, band_order):
    feed, band = lax.axis_index("feed"), lax.axis_index("band")
    half = (feed // 2) % 2
    low = band < 2
    everyone = (0, 1, 2, 3)

    gains = feed_gains.reshape(2, 16, 2, 16, 256)
    other_gain = lax.dynamic_index_in_dim(gains, 1 - half, 2, keepdims=False)
    other_gain = lax.ppermute(other_gain, BOTH, hop(4, everyone))
    own_weights = beam_weights[:, 0]
    away = lax.dynamic_slice_in_dim(own_weights, jnp.where(low, 512, 0), 512, 1)
    near = lax.ppermute(away, BOTH, hop(1, (1,)) + hop(-1, (2,)))
    far = lax.ppermute(away, BOTH, hop(2, (0,)) + hop(-2, (3,)))
    end = lax.dynamic_slice_in_dim(own_weights, jnp.where(low, 256, 512), 256, 1)
    end = lax.ppermute(end, BOTH, hop(1, (0,)) + hop(-1, (3,)))

    sections = []
    for start in (0, 2):
        spectra = channelize(start, voltages, filter_taps, band_order)
        got = lax.all_to_all(spectra, "feed", 0, 0, axis_index_groups=PLANE_GROUPS, tiled=True)
        own, other = calibrate(half, got, gains, other_gain)
        up = [jnp.where(low, own, other)]
        down = [jnp.where(low, other, own)]
        for senders in (everyone, everyone, (0, 1, 2), (1, 2)):
            up.append(lax.ppermute(up[-1], BOTH, hop(1, senders)))
            down.append(lax.ppermute(down[-1], BOTH, hop(-1, tuple(3 - p for p in senders))))
        same, swap = half, 1 - half
        table = (
            (own, ((0, same), (1, same), (2, same), (3, same))),
            (up[1], ((3, swap), (0, same), (1, same), (2, swap))),
            (down[1], ((1, swap), (2, same), (3, same), (0, swap))),
            (up[2], ((2, swap), (3, swap), (0, same), (1, same))),
            (down[2], ((2, same), (3, same), (0, swap), (1, swap))),
            (up[3], ((1, same), (2, swap), (3, swap), (0, same))),
            (down[3], ((3, same), (0, swap), (1, swap), (2, same))),
            (jnp.where(low, down[4], up[4]), ((0, swap), (1, swap), (2, swap), (3, swap))),
        )
        section = jnp.zeros((4, 16, 2, 16, 1024), BF16)
        for unit, places in table:
            group = jnp.stack([jnp.int32(g) for g, _ in places])[band]
            part = jnp.stack([p for _, p in places])[band]
            section = lax.dynamic_update_slice(
                section, unit.reshape(1, 16, 1, 16, 1024), (group, 0, part, 0, 0)
            )
        sections.append(section.reshape(2048, 1024))

    average = 1.0 / 1024
    outer = jnp.where(low, 0, 3)
    weights = weight_rows(band, beam_mask, own_weights, near, far, end)
    inward = hop(-1, (1,)) + hop(1, (2,))
    block = pairs(average, outer, band, 1, 512, sections)
    block = lax.ppermute(block, BOTH, inward)
    share = jnp.stack([beams(1, weights, section, BF16) for section in sections])
    share = lax.ppermute(share, BOTH, inward)

    visibility = pairs(average, band, jnp.int32(0), 4, 512, sections)
    formed = jnp.stack([beams(0, weights, section, F32) for section in sections])
    is_outer = (band == 0) | (band == 3)
    where = jnp.where(low, 1, 2) * 512
    kept = lax.dynamic_slice_in_dim(visibility, where, 512, 2)
    visibility = lax.dynamic_update_slice_in_dim(visibility, jnp.where(is_outer, block, kept), where, 2)
    formed = formed + jnp.where(is_outer, share.astype(F32), 0.0)
    formed = formed.astype(BF16).reshape(2, 256, 2, 2, 256).transpose(1, 2, 0, 3, 4)
    return (visibility[:, None], formed.reshape(1, 256, 2, 4, 256))


def solution(mesh):
    return jax.shard_map(
        shards,
        mesh=mesh,
        in_specs=(
            P(None, ("band", "feed"), None),
            P(),
            P(None, "feed", "band", None),
            P(None, "feed", None, "band"),
            P(),
            P(),
        ),
        out_specs=(P(None, "feed", "band", None), P("feed", "band", None, None, None)),
        check_vma=False,
    )
```

```python
import math

import jax
import jax.numpy as jnp
import numpy as np
from jax import lax
from jax.experimental import pallas as pl
from jax.experimental.pallas import tpu as pltpu
from jax.sharding import PartitionSpec as P

RADIX = 128
TILE = 32
SIDE = 4
BOTH = ("feed", "band")
F32 = jnp.float32
BF16 = jnp.bfloat16


def feed_at(y, x, half, core):
    return ((y * SIDE + x) * 2 + half) * 2 + core


PLANE_GROUPS = [
    [feed_at(y, x, half, core) for y in range(SIDE) for x in range(SIDE) for core in range(2)]
    for half in range(2)
]


def hop(step, senders):
    pairs = []
    for y in range(SIDE):
        for x in range(SIDE):
            for core in range(2):
                for z in range(8):
                    if z % 4 in senders:
                        to = (z + step) % 8
                        pairs.append(
                            (feed_at(y, x, z // 4, core) * 4 + z % 4, feed_at(y, x, to // 4, core) * 4 + to % 4)
                        )
    return pairs


def constants(length):
    row = np.arange(RADIX)
    angles = (row[:, None] * row[None, :] % RADIX) * (2.0 * math.pi / RADIX)
    factor = 1.0 / math.sqrt(RADIX)
    re = (np.cos(angles) * factor).astype(np.float32)
    im = (-np.sin(angles) * factor).astype(np.float32)
    first = np.block([[re, -im], [im, re]])
    second = np.stack([np.hstack([re, -im]), np.hstack([im, re])])
    second = second.reshape(2, RADIX // 2, 2, 2 * RADIX).transpose(0, 2, 1, 3).reshape(2 * RADIX, 2 * RADIX)
    twiddle = (row[:, None] * row[None, :] % length) * (2.0 * math.pi / length)
    tw = np.stack([np.cos(twiddle), -np.sin(twiddle)]).astype(np.float32)
    place = np.zeros((64, 2 * RADIX), np.float32)
    for yx in range(16):
        for core in range(2):
            for half in range(2):
                place[(yx * 2 + core) * 2 + half, (yx * 2 + half) * 2 + core] = 1.0
    return (jnp.asarray(np.concatenate([first, second, place]), BF16), jnp.asarray(tw))


def channel_kernel(order_ref, tables_hbm, tw_hbm, taps_hbm, volts_hbm, out_ref, frame, turned, lhs, tables, tw_ref, taps_ref, volts_ref, sems):
    length = taps_ref.shape[1]
    early, late = pl.ds(0, 5 * length), pl.ds(5 * length, 2 * length)
    copies = [
        pltpu.make_async_copy(tables_hbm, tables, sems.at[0]),
        pltpu.make_async_copy(taps_hbm, taps_ref, sems.at[1]),
        pltpu.make_async_copy(volts_hbm.at[:, :, early], volts_ref.at[:, :, early], sems.at[2]),
        pltpu.make_async_copy(tw_hbm, tw_ref, sems.at[3]),
        pltpu.make_async_copy(volts_hbm.at[:, :, late], volts_ref.at[:, :, late], sems.at[4]),
    ]
    for copy in copies:
        copy.start()
    pick = (order_ref[...] == lax.broadcasted_iota(jnp.int32, (64, 64), 0)).astype(BF16)
    copies[0].wait()
    pick = lax.dot_general(tables[512:576, :64], pick, BOTH_LAST, preferred_element_type=F32).astype(BF16)
    for part in range(4):
        second = tables[256 + part * 64 : 256 + (part + 1) * 64, :]
        lhs[part * 64 : (part + 1) * 64, :] = jnp.dot(pick, second, preferred_element_type=F32).astype(BF16)
    width = 16 * RADIX
    for copy in copies[1:4]:
        copy.wait()
    for start in (0, 2):
        if start:
            copies[4].wait()

        def filter_chunk(chunk, carry):
            lane = pl.multiple_of(chunk * width, width)
            taps = [jnp.broadcast_to(taps_ref[t : t + 1, pl.ds(lane, width)], (8, width)) for t in range(4)]
            for part in range(2):
                volts = [volts_ref[part, :, pl.ds((start + n) * length + lane, width)].astype(F32) for n in range(5)]
                for s in range(2):
                    total = taps[0] * volts[s]
                    for t in range(1, 4):
                        total = total + taps[t] * volts[s + t]
                    for a in range(16):
                        at = pl.multiple_of(chunk * width // RADIX * 8 + a * 8, 8)
                        frame[s, part, pl.ds(at, 8), :] = total[:, a * RADIX : (a + 1) * RADIX]
            return carry

        lax.fori_loop(0, length // width, filter_chunk, 0)
        tw_re, tw_im = tw_ref[0], tw_ref[1]
        for f in range(8):
            columns = []
            for s in range(2):
                parts = [frame[s, part, pl.ds(f, RADIX, stride=8), :] for part in range(2)]
                columns.append(jnp.concatenate(parts, axis=0))
            values = jnp.concatenate(columns, axis=1).astype(BF16)
            mid = jnp.dot(tables[:256, :], values, preferred_element_type=F32)
            rows = []
            for s in range(2):
                re = mid[:RADIX, s * RADIX : (s + 1) * RADIX]
                im = mid[RADIX:, s * RADIX : (s + 1) * RADIX]
                rows.append(jnp.concatenate([re * tw_re - im * tw_im, re * tw_im + im * tw_re], axis=1).astype(BF16))
            rotated = jnp.concatenate(rows, axis=0)
            out = lax.dot_general(lhs[...], rotated, BOTH_LAST, preferred_element_type=F32)
            for part in range(2):
                for h in range(2):
                    for s in range(2):
                        at = part * RADIX + h * 64
                        columns = out[at : at + 64, s * RADIX : (s + 1) * RADIX]
                        turned[s * 4 + part * 2 + h, pl.ds(f, 64, stride=8), :] = columns
        for block in range(8):
            at = start * 512 + block * RADIX
            out_ref[:, :, at : at + RADIX] = turned[block].reshape(32, 16, RADIX).astype(BF16)


ANY = pl.BlockSpec(memory_space=pl.ANY)
VMEM = pl.BlockSpec(memory_space=pltpu.VMEM)
SMEM = pl.BlockSpec(memory_space=pltpu.SMEM)
GRANT = pltpu.CompilerParams(vmem_limit_bytes=56 * 2**20)
BRIEF = pl.CostEstimate(flops=1, bytes_accessed=1, transcendentals=0)


BOTH_LAST = (((1,), (1,)), ((), ()))


def channelize(voltages, filter_taps, band_order):
    tables, tw = constants(filter_taps.shape[1])
    return pl.pallas_call(
        channel_kernel,
        out_shape=jax.ShapeDtypeStruct((32, 16, 2048), BF16),
        in_specs=[VMEM] + [ANY] * 4,
        out_specs=VMEM,
        scratch_shapes=[
            pltpu.VMEM((2, 2, 8 * RADIX, RADIX), F32),
            pltpu.VMEM((8, 512, RADIX), F32),
            pltpu.VMEM((256, 256), BF16),
            pltpu.VMEM(tables.shape, BF16),
            pltpu.VMEM(tw.shape, F32),
            pltpu.VMEM(filter_taps.shape, F32),
            pltpu.VMEM(voltages.shape, BF16),
            pltpu.SemaphoreType.DMA((5,)),
        ],
        compiler_params=GRANT,
        cost_estimate=BRIEF,
        name="channelize",
    )(band_order.reshape(1, 64), tables, tw, filter_taps, voltages)


def times(gain, values):
    parts = []
    for at in range(0, values.shape[-1], 512):
        re, im = values[:, at : at + 256], values[:, at + 256 : at + 512]
        parts += [gain[0] * re - gain[1] * im, gain[0] * im + gain[1] * re]
    return jnp.concatenate(parts, axis=1)


def calibrate_kernel(at_ref, got_ref, gain_ref, up_ref, down_ref):
    half, low_band = at_ref[0], at_ref[1] < 2
    got = got_ref[...].astype(F32)
    swapped = half == 1
    own = jnp.where(swapped, got[:, 8:], got[:, :8]).reshape(256, got.shape[2])
    other = jnp.where(swapped, got[:, :8], got[:, 8:]).reshape(256, got.shape[2])
    own = times(gain_ref[:, :, half].astype(F32).reshape(2, 256, 256), own)
    up_ref[...] = jnp.where(low_band, own, other).astype(BF16)
    down_ref[...] = jnp.where(low_band, other, own).astype(BF16)


def calibrate(section, place, got, gains):
    return pl.pallas_call(
        calibrate_kernel,
        out_shape=[jax.ShapeDtypeStruct((256, 1024), BF16)] * 2,
        grid=(1,),
        in_specs=[
            SMEM,
            pl.BlockSpec((32, 16, 1024), lambda i: (0, 0, section)),
            pl.BlockSpec((2, 16, 2, 16, 256), lambda i: (0, 0, 0, 0, 0)),
        ],
        out_specs=[pl.BlockSpec((256, 1024), lambda i: (0, 0))] * 2,
        compiler_params=GRANT,
        cost_estimate=BRIEF,
        name="calibrate",
    )(place, got, gains)


def enter_kernel(at_ref, part_hbm, gain_hbm, out_hbm, part, gain, sems):
    @pl.when(at_ref[0] == 1)
    def _():
        loads = [pltpu.make_async_copy(part_hbm, part, sems.at[0]), pltpu.make_async_copy(gain_hbm, gain, sems.at[1])]
        for copy in loads:
            copy.start()
        for copy in loads:
            copy.wait()
        part[...] = times(gain[...].astype(F32).reshape(2, 256, 256), part[...].astype(F32)).astype(BF16)
        store = pltpu.make_async_copy(part, out_hbm, sems.at[2])
        store.start()
        store.wait()


def enter(is_entry, part, gain):
    return pl.pallas_call(
        enter_kernel,
        out_shape=jax.ShapeDtypeStruct(part.shape, BF16),
        in_specs=[SMEM, ANY, ANY],
        out_specs=ANY,
        scratch_shapes=[
            pltpu.VMEM(part.shape, BF16),
            pltpu.VMEM(gain.shape, BF16),
            pltpu.SemaphoreType.DMA((3,)),
        ],
        input_output_aliases={1: 0},
        compiler_params=GRANT,
        cost_estimate=BRIEF,
        name="enter",
    )(is_entry.astype(jnp.int32).reshape(1), part, gain)


def spread(mask, group):
    tile = lax.broadcasted_iota(jnp.int32, (64, 512), 0)
    column = lax.broadcasted_iota(jnp.int32, (64, 512), 1) // TILE + group * 16
    return jnp.dot(mask, (tile == column).astype(BF16), preferred_element_type=F32).astype(BF16)


def weights_kernel(at_ref, mask_ref, local_ref, near_ref, far_ref, end_ref, out_ref):
    band = at_ref[0]
    low = band < 2
    groups = (band, jnp.where(low, 2, 1), jnp.where(low, 3, 0), jnp.where(low, 1 - band, 5 - band))
    mask = mask_ref[...].astype(F32).astype(BF16)
    for group, src_ref in zip(groups, (local_ref, near_ref, far_ref, end_ref)):
        lanes = pl.ds(pl.multiple_of(group * 512, 512), 512)
        wide = spread(mask, group)
        for part in range(2):
            out_ref[part * 256 : (part + 1) * 256, lanes] = src_ref[part] * wide


def weight_rows(band, mask, local, *others):
    fixed = pl.BlockSpec((2, 256, 512), lambda i, at: (0, 0, 0))
    return pl.pallas_call(
        weights_kernel,
        out_shape=jax.ShapeDtypeStruct((512, 2048), BF16),
        grid_spec=pltpu.PrefetchScalarGridSpec(
            num_scalar_prefetch=1,
            grid=(1,),
            in_specs=[
                pl.BlockSpec((256, 64), lambda i, at: (at[0], 0)),
                pl.BlockSpec((2, 256, 512), lambda i, at: (0, at[0], 0)),
            ]
            + [fixed] * 3,
            out_specs=pl.BlockSpec((512, 2048), lambda i, at: (0, 0)),
        ),
        compiler_params=GRANT,
        cost_estimate=BRIEF,
        name="weight_rows",
    )(band.reshape(1), mask, local, *others)


def crossed(left):
    parts = []
    for at in range(0, left.shape[1], 512):
        parts += [left[:, at + 256 : at + 512], -left[:, at : at + 256]]
    return jnp.concatenate(parts, axis=1)


def fetch(low, half, sources, to, sems):
    waits = []
    for index, (below, above) in enumerate(sources):
        place = to.at[:, half if index == 0 else 1 - half]
        copies = [pltpu.make_async_copy(ref, place, sems.at[index]) for ref in (below, above)]
        pl.when(low)(copies[0].start)
        pl.when(jnp.logical_not(low))(copies[1].start)
        waits.append(copies[0])
    return waits


def weighted(mask, group, weight_ref, values):
    wide = spread(mask, group)
    both = jnp.concatenate([weight_ref[0] * wide, weight_ref[1] * wide], axis=0)
    total = jnp.dot(both, values, preferred_element_type=F32)
    parts = []
    for at in range(0, values.shape[1], 512):
        re, im = slice(at, at + 256), slice(at + 256, at + 512)
        parts += [total[:256, re] - total[256:, im], total[:256, im] + total[256:, re]]
    return jnp.concatenate(parts, axis=1)


def gather(half, band, sources, to, sems):
    low = band < 2
    same, swap = half, 1 - half
    up_0, down_0, up_1, down_1, up_2, down_2, up_3, down_3, up_4, down_4 = sources
    table = (
        (up_0, down_0, ((0, same), (1, same), (2, same), (3, same))),
        (up_1, up_1, ((3, swap), (0, same), (1, same), (2, swap))),
        (down_1, down_1, ((1, swap), (2, same), (3, same), (0, swap))),
        (up_2, up_2, ((2, swap), (3, swap), (0, same), (1, same))),
        (down_2, down_2, ((2, same), (3, same), (0, swap), (1, swap))),
        (up_3, up_3, ((1, same), (2, swap), (3, swap), (0, same))),
        (down_3, down_3, ((3, same), (0, swap), (1, swap), (2, same))),
        (down_4, up_4, ((0, swap), (1, swap), (2, swap), (3, swap))),
    )
    waits = []
    for index, (below, above, places) in enumerate(table):
        group = by_band(band, [g for g, _ in places])
        run = by_band(band, [r for _, r in places])
        copies = [pltpu.make_async_copy(ref, to.at[group, :, run], sems.at[index]) for ref in (below, above)]
        pl.when(low)(copies[0].start)
        pl.when(jnp.logical_not(low))(copies[1].start)
        waits.append(copies[0])
    return waits


def share_kernel(at_ref, mask_ref, near_weight, far_weight, *refs):
    sources, out_ref, near, far, sems = refs[:8], refs[8], refs[9], refs[10], refs[11]
    half, band = at_ref[0], at_ref[1]
    low = band < 2
    near_waits = fetch(low, half, (sources[0:2], sources[2:4]), near, sems.at[0])
    far_waits = fetch(low, half, (sources[4:6], sources[6:8]), far, sems.at[1])
    mask = mask_ref[...].astype(F32).astype(BF16)
    for copy in near_waits:
        copy.wait()
    total = weighted(mask, jnp.where(low, 2, 1), near_weight, near[...].reshape(512, 1024))
    for copy in far_waits:
        copy.wait()
    out_ref[...] = total + weighted(mask, jnp.where(low, 3, 0), far_weight, far[...].reshape(512, 1024))


def outer_rows(at):
    return jnp.where(at[1] < 2, 0, 3)


def early_share(place, mask, near_weight, far_weight, parts):
    fixed = pl.BlockSpec((2, 256, 512), lambda i, at: (0, 0, 0))
    return pl.pallas_call(
        share_kernel,
        out_shape=jax.ShapeDtypeStruct((256, 1024), F32),
        grid_spec=pltpu.PrefetchScalarGridSpec(
            num_scalar_prefetch=1,
            grid=(1,),
            in_specs=[pl.BlockSpec((256, 64), lambda i, at: (outer_rows(at), 0)), fixed, fixed] + [ANY] * 8,
            out_specs=pl.BlockSpec((256, 1024), lambda i, at: (0, 0)),
            scratch_shapes=[pltpu.VMEM((16, 2, 16, 1024), BF16)] * 2 + [pltpu.SemaphoreType.DMA((2, 2))],
        ),
        compiler_params=GRANT,
        cost_estimate=BRIEF,
        name="early_share",
    )(place, mask, near_weight, far_weight, *[part.reshape(16, 16, 1024) for part in parts])


def edge_kernel(average, summed, at_ref, mask_ref, weight_ref, early_ref, *refs):
    sources, (block_ref, share_ref, rows, cols, sems) = refs[:8], refs[-5:]
    so_far = refs[8:9] if summed else ()
    half, band = at_ref[0], at_ref[1]
    low = band < 2
    col_waits = fetch(low, half, (sources[4:6], sources[6:8]), cols, sems.at[0])
    row_waits = fetch(low, half, (sources[0:2], sources[2:4]), rows, sems.at[1])
    mask = mask_ref[...].astype(F32).astype(BF16)
    for copy in col_waits:
        copy.wait()
    right = cols[...].reshape(512, 1024)
    share_ref[...] = (early_ref[...] + weighted(mask, band, weight_ref, right)).astype(BF16)
    for copy in row_waits:
        copy.wait()
    left = rows[...].reshape(512, 1024)
    both = jnp.concatenate([left, crossed(left)], axis=0)
    total = lax.dot_general(both, right, BOTH_LAST, preferred_element_type=F32)
    if so_far:
        total = total + so_far[0][...]
        block_ref[0] = (total[:512] * average).astype(BF16)
        block_ref[1] = (total[512:] * average).astype(BF16)
    else:
        block_ref[...] = total


def edge(average, place, mask, local, early, parts, so_far, after):
    block = jax.ShapeDtypeStruct((2, 512, 512), BF16) if so_far else jax.ShapeDtypeStruct((1024, 512), F32)
    whole = lambda shape: pl.BlockSpec(shape, lambda i, at: (0,) * len(shape))
    return pl.pallas_call(
        lambda *refs: edge_kernel(average, bool(so_far), *refs),
        out_shape=[block, jax.ShapeDtypeStruct((256, 1024), BF16)],
        grid_spec=pltpu.PrefetchScalarGridSpec(
            num_scalar_prefetch=1,
            grid=(1,),
            in_specs=[
                pl.BlockSpec((256, 64), lambda i, at: (outer_rows(at), 0)),
                pl.BlockSpec((2, 256, 512), lambda i, at: (0, outer_rows(at), 0)),
                whole((256, 1024)),
            ]
            + [ANY] * 8
            + [whole((1024, 512))] * len(so_far)
            + [ANY] * len(after),
            out_specs=[whole(block.shape), whole((256, 1024))],
            scratch_shapes=[pltpu.VMEM((16, 2, 16, 1024), BF16)] * 2 + [pltpu.SemaphoreType.DMA((2, 2))],
        ),
        compiler_params=GRANT,
        cost_estimate=BRIEF,
        name="edge",
    )(place, mask, local, early, *[part.reshape(16, 16, 1024) for part in parts], *so_far, *after)


def given_group(band):
    return jnp.where(band < 2, 1, 2)


def pair_kernel(average, at_ref, *refs):
    sources, (out_ref, section_a, section_b, held, lhs, made, sems, out_sems) = refs[:20], refs[-8:]
    half, band = at_ref[0], at_ref[1]
    waits = []
    for index in range(2):
        waits += gather(half, band, sources[index * 10 : (index + 1) * 10], held.at[index], sems.at[index])
    for copy in waits:
        copy.wait()
    kept = [pltpu.make_async_copy(held.at[i], to, out_sems.at[i]) for i, to in enumerate((section_a, section_b))]
    for copy in kept:
        copy.start()
    for index in range(2):
        left = held[index, band].reshape(512, 1024)
        lhs[:512, index * 1024 : (index + 1) * 1024] = left
        lhs[512:, index * 1024 : (index + 1) * 1024] = crossed(left)
    stores = []
    for step in range(3):
        group = step + (step >= given_group(band)).astype(jnp.int32)
        total = None
        for index in range(2):
            right = held[index, group].reshape(512, 1024)
            now = lax.dot_general(
                lhs[:, index * 1024 : (index + 1) * 1024], right, BOTH_LAST, preferred_element_type=F32
            )
            total = now if total is None else total + now
        made[step, 0] = (total[:512] * average).astype(BF16)
        made[step, 1] = (total[512:] * average).astype(BF16)
        lanes = pl.ds(pl.multiple_of(group * 512, 512), 512)
        stores.append(pltpu.make_async_copy(made.at[step], out_ref.at[:, :, lanes], out_sems.at[2 + step]))
        stores[-1].start()
    for copy in kept + stores:
        copy.wait()


def pairs(average, place, ups, downs, *after):
    parts = []
    for up, down in zip(ups, downs):
        parts += [part.reshape(16, 16, 1024) for pair in zip(up, down) for part in pair]
    section = jax.ShapeDtypeStruct((4, 16, 2, 16, 1024), BF16)
    visibility, *sections = pl.pallas_call(
        lambda *refs: pair_kernel(average, *refs),
        out_shape=[jax.ShapeDtypeStruct((2, 512, 2048), BF16), section, section],
        in_specs=[SMEM] + [ANY] * (20 + len(after)),
        out_specs=[ANY] * 3,
        scratch_shapes=[
            pltpu.VMEM((2, 4, 16, 2, 16, 1024), BF16),
            pltpu.VMEM((1024, 2048), BF16),
            pltpu.VMEM((3, 2, 512, 512), BF16),
            pltpu.SemaphoreType.DMA((2, 8)),
            pltpu.SemaphoreType.DMA((5,)),
        ],
        compiler_params=GRANT,
        cost_estimate=BRIEF,
        name="pairs",
    )(place, *parts, *after)
    return visibility, [section.reshape(2048, 1024) for section in sections]


def last_kernel(average, at_ref, left_a, left_b, right_a, right_b, block_ref, whole_ref, out_ref, lhs):
    band = at_ref[0]
    is_outer = (band == 0) | (band == 3)

    @pl.when(is_outer)
    def _():
        out_ref[...] = block_ref[...]

    @pl.when(jnp.logical_not(is_outer))
    def _():
        total = None
        for left_ref, right_ref in ((left_a, right_a), (left_b, right_b)):
            lhs[:512, :] = left_ref[...]
            lhs[512:, :] = crossed(left_ref[...])
            now = lax.dot_general(lhs[...], right_ref[...], BOTH_LAST, preferred_element_type=F32)
            total = now if total is None else total + now
        out_ref[0] = (total[:512] * average).astype(BF16)
        out_ref[1] = (total[512:] * average).astype(BF16)


def last_pairs(average, band, sections, block, visibility):
    left = pl.BlockSpec((512, 1024), lambda i, at: (at[0], 0))
    right = pl.BlockSpec((512, 1024), lambda i, at: (given_group(at[0]), 0))
    return pl.pallas_call(
        lambda *refs: last_kernel(average, *refs),
        out_shape=jax.ShapeDtypeStruct((2, 512, 2048), BF16),
        grid_spec=pltpu.PrefetchScalarGridSpec(
            num_scalar_prefetch=1,
            grid=(1,),
            in_specs=[left, left, right, right, pl.BlockSpec((2, 512, 512), lambda i, at: (0, 0, 0)), ANY],
            out_specs=pl.BlockSpec((2, 512, 512), lambda i, at: (0, 0, given_group(at[0]))),
            scratch_shapes=[pltpu.VMEM((1024, 1024), BF16)],
        ),
        input_output_aliases={6: 0},
        compiler_params=GRANT,
        cost_estimate=BRIEF,
        name="last_pairs",
    )(band.reshape(1), sections[0], sections[1], sections[0], sections[1], block, visibility)


def beam_kernel(weight_ref, section_a, section_b, out_ref):
    step = pl.program_id(0)

    def form(section_ref):
        total = jnp.dot(weight_ref[...], section_ref[...], preferred_element_type=F32)
        out_ref[:, :256] = (total[:256, :256] - total[256:, 256:]).astype(out_ref.dtype)
        out_ref[:, 256:] = (total[:256, 256:] + total[256:, :256]).astype(out_ref.dtype)

    pl.when(step < 2)(lambda: form(section_a))
    pl.when(step >= 2)(lambda: form(section_b))


def beams(weights, sections, dtype):
    formed = pl.pallas_call(
        beam_kernel,
        out_shape=jax.ShapeDtypeStruct((256, 2048), dtype),
        grid=(4,),
        in_specs=[
            pl.BlockSpec((512, 2048), lambda i: (0, 0)),
            pl.BlockSpec((2048, 512), lambda i: (0, jnp.minimum(i, 1))),
            pl.BlockSpec((2048, 512), lambda i: (0, jnp.maximum(i - 2, 0))),
        ],
        out_specs=pl.BlockSpec((256, 512), lambda i: (0, i)),
        compiler_params=GRANT,
        cost_estimate=BRIEF,
        name="beams",
    )(weights, *sections)
    return formed


def finish_kernel(at_ref, formed_ref, share_a, share_b, *refs):
    out_ref, turned = refs[-2:]
    is_outer = (at_ref[1] == 0) | (at_ref[1] == 3)
    for spectrum in range(4):
        share_ref = (share_a, share_b)[spectrum // 2]
        for part in range(2):
            at = spectrum * 512 + part * 256
            total = formed_ref[:, at : at + 256]
            at = at % 1024
            total = total + jnp.where(is_outer, share_ref[:, at : at + 256].astype(F32), 0.0)
            for lane in range(2):
                turned[lane, pl.ds(part * 4 + spectrum, 256, stride=8), :] = total[:, lane * 128 : (lane + 1) * 128]
    for lane in range(2):
        out_ref[:, lane * 128 : (lane + 1) * 128] = turned[lane].astype(BF16)


def finish(place, formed, shares, *after):
    return pl.pallas_call(
        finish_kernel,
        out_shape=jax.ShapeDtypeStruct((2048, 256), BF16),
        in_specs=[SMEM] + [VMEM] * 3 + [ANY] * len(after),
        out_specs=VMEM,
        scratch_shapes=[pltpu.VMEM((2, 2048, 128), F32)],
        compiler_params=GRANT,
        cost_estimate=BRIEF,
        name="finish",
    )(place, formed, *shares, *after)


def by_band(band, values):
    first, second, third, fourth = values
    return jnp.where(band < 2, jnp.where(band == 0, first, second), jnp.where(band == 2, third, fourth))


def shards(voltages, filter_taps, feed_gains, beam_weights, beam_mask, band_order):
    feed, band = lax.axis_index("feed"), lax.axis_index("band")
    half = lax.shift_right_logical(feed, 1) & 1
    low = band < 2
    outer = jnp.where(low, 0, 3)
    is_outer = band == outer
    everyone = (0, 1, 2, 3)
    place = jnp.stack([half, band])

    gains = feed_gains.reshape(2, 16, 2, 16, 256)
    sent_gain = lax.dynamic_index_in_dim(gains, 1 - half, 2, keepdims=False)
    entry_gains = (
        lax.ppermute(sent_gain, BOTH, hop(-3, (3,)) + hop(3, (0,))),
        lax.ppermute(sent_gain, BOTH, hop(-2, (2,)) + hop(2, (1,))),
    )
    own_weights = beam_weights[:, 0]
    from_near, from_far, from_end = hop(1, (1,)) + hop(-1, (2,)), hop(2, (0,)) + hop(-2, (3,)), hop(1, (0,)) + hop(-1, (3,))
    away = lax.dynamic_slice_in_dim(own_weights, jnp.where(low, 768, 0), 256, 1)
    near_outer = lax.ppermute(away, BOTH, from_near)
    far_outer = lax.ppermute(away, BOTH, from_far)

    spectra = channelize(voltages, filter_taps, band_order)
    got = lax.all_to_all(spectra, "feed", 0, 0, axis_index_groups=PLANE_GROUPS, tiled=True)
    got, near_outer, *entry_gains = lax.optimization_barrier((got, near_outer) + entry_gains)
    entry_gains[1], far_outer = lax.optimization_barrier((entry_gains[1], far_outer))
    ups, downs = [], []
    earlies = []
    for section in range(2):
        up, down = ([part] for part in calibrate(section, place, got, gains))
        for step, senders in enumerate((everyone, everyone, (0, 1, 2), (1, 2))):
            if step == 3:
                if earlies:
                    up[3], _ = lax.optimization_barrier((up[3], earlies[0]))
                across = (down[1], up[1], up[3], down[3], down[2], up[2], up[2], down[2])
                earlies.append(early_share(place, beam_mask, near_outer, far_outer, across))
            up.append(lax.ppermute(up[-1], BOTH, hop(1, senders)))
            down.append(lax.ppermute(down[-1], BOTH, hop(-1, tuple(3 - p for p in senders))))
            if step < 2:
                up[-1] = enter(band == 0, up[-1], entry_gains[step])
                down[-1] = enter(band == 3, down[-1], entry_gains[step])
        ups.append(up)
        downs.append(down)

    average = 1.0 / 1024
    inward = hop(-1, (1,)) + hop(1, (2,))
    so_far, shares = (), []
    for up, down, early in zip(ups, downs, earlies):
        beside = (up[1], down[1], down[3], up[3], up[0], down[0], down[4], up[4])
        after = () if so_far else (earlies[1],)
        block, share = edge(average, place, beam_mask, own_weights, early, beside, so_far, after)
        so_far = (block,)
        shares.append(lax.ppermute(share, BOTH, inward))
    received = lax.ppermute(block, BOTH, inward)


    late, _, _ = lax.optimization_barrier((own_weights, block, shares[0]))
    away = lax.dynamic_slice_in_dim(late, jnp.where(low, 512, 256), 256, 1)
    near = lax.ppermute(away, BOTH, from_near)
    far = lax.ppermute(away, BOTH, from_far)
    away = lax.dynamic_slice_in_dim(late, jnp.where(low, 256, 512), 256, 1)
    end = lax.ppermute(away, BOTH, from_end)

    visibility, sections = pairs(average, place, ups, downs, block, shares[0])
    visibility = last_pairs(average, band, sections, received, visibility)
    own_rows = weight_rows(band, beam_mask, own_weights, near, far, end)
    formed = finish(place, beams(own_rows, sections, F32), shares, visibility)
    return (visibility[:, None], formed.reshape(1, 256, 2, 4, 256))


def solution(mesh):
    return jax.shard_map(
        shards,
        mesh=mesh,
        in_specs=(
            P(None, ("band", "feed"), None),
            P(),
            P(None, "feed", "band", None),
            P(None, "feed", None, "band"),
            P(),
            P(),
        ),
        out_specs=(P(None, "feed", "band", None), P("feed", "band", None, None, None)),
        check_vma=False,
    )
```

```python
import math

import jax
import jax.numpy as jnp
import numpy as np
from jax import lax
from jax.experimental import pallas as pl
from jax.experimental.pallas import tpu as pltpu
from jax.sharding import PartitionSpec as P

RADIX = 128
TILE = 32
SIDE = 4
BOTH = ("feed", "band")
F32 = jnp.float32
BF16 = jnp.bfloat16


def feed_at(y, x, half, core):
    return ((y * SIDE + x) * 2 + half) * 2 + core


PLANE_GROUPS = [
    [feed_at(y, x, half, core) for y in range(SIDE) for x in range(SIDE) for core in range(2)]
    for half in range(2)
]


def hop(step, senders):
    pairs = []
    for y in range(SIDE):
        for x in range(SIDE):
            for core in range(2):
                for z in range(8):
                    if z % 4 in senders:
                        to = (z + step) % 8
                        pairs.append(
                            (feed_at(y, x, z // 4, core) * 4 + z % 4, feed_at(y, x, to // 4, core) * 4 + to % 4)
                        )
    return pairs


def constants(length):
    row = np.arange(RADIX)
    angles = (row[:, None] * row[None, :] % RADIX) * (2.0 * math.pi / RADIX)
    factor = 1.0 / math.sqrt(RADIX)
    re = (np.cos(angles) * factor).astype(np.float32)
    im = (-np.sin(angles) * factor).astype(np.float32)
    first = np.block([[re, -im], [im, re]])
    second = np.stack([np.hstack([re, -im]), np.hstack([im, re])])
    second = second.reshape(2, RADIX // 2, 2, 2 * RADIX).transpose(0, 2, 1, 3).reshape(2 * RADIX, 2 * RADIX)
    twiddle = (row[:, None] * row[None, :] % length) * (2.0 * math.pi / length)
    tw = np.stack([np.cos(twiddle), -np.sin(twiddle)]).astype(np.float32)
    place = np.zeros((64, 2 * RADIX), np.float32)
    for yx in range(16):
        for core in range(2):
            for half in range(2):
                place[(yx * 2 + core) * 2 + half, (yx * 2 + half) * 2 + core] = 1.0
    return (jnp.asarray(np.concatenate([first, second, place]), BF16), jnp.asarray(tw))


def channel_kernel(order_ref, tables_hbm, tw_hbm, taps_hbm, volts_hbm, out_ref, frame, turned, lhs, tables, tw_ref, taps_ref, volts_ref, sems):
    length = taps_ref.shape[1]
    early, late = pl.ds(0, 5 * length), pl.ds(5 * length, 2 * length)
    copies = [
        pltpu.make_async_copy(tables_hbm, tables, sems.at[0]),
        pltpu.make_async_copy(taps_hbm, taps_ref, sems.at[1]),
        pltpu.make_async_copy(volts_hbm.at[:, :, early], volts_ref.at[:, :, early], sems.at[2]),
        pltpu.make_async_copy(tw_hbm, tw_ref, sems.at[3]),
        pltpu.make_async_copy(volts_hbm.at[:, :, late], volts_ref.at[:, :, late], sems.at[4]),
    ]
    for copy in copies:
        copy.start()
    pick = (order_ref[...] == lax.broadcasted_iota(jnp.int32, (64, 64), 0)).astype(BF16)
    copies[0].wait()
    pick = lax.dot_general(tables[512:576, :64], pick, BOTH_LAST, preferred_element_type=F32).astype(BF16)
    for part in range(4):
        second = tables[256 + part * 64 : 256 + (part + 1) * 64, :]
        lhs[part * 64 : (part + 1) * 64, :] = jnp.dot(pick, second, preferred_element_type=F32).astype(BF16)
    width = 16 * RADIX
    for copy in copies[1:4]:
        copy.wait()
    for start in (0, 2):
        if start:
            copies[4].wait()

        def filter_chunk(chunk, carry):
            lane = pl.multiple_of(chunk * width, width)
            taps = [jnp.broadcast_to(taps_ref[t : t + 1, pl.ds(lane, width)], (8, width)) for t in range(4)]
            for part in range(2):
                volts = [volts_ref[part, :, pl.ds((start + n) * length + lane, width)].astype(F32) for n in range(5)]
                for s in range(2):
                    total = taps[0] * volts[s]
                    for t in range(1, 4):
                        total = total + taps[t] * volts[s + t]
                    for a in range(16):
                        at = pl.multiple_of(chunk * width // RADIX * 8 + a * 8, 8)
                        frame[s, part, pl.ds(at, 8), :] = total[:, a * RADIX : (a + 1) * RADIX]
            return carry

        lax.fori_loop(0, length // width, filter_chunk, 0)
        tw_re, tw_im = tw_ref[0], tw_ref[1]
        for f in range(8):
            columns = []
            for s in range(2):
                parts = [frame[s, part, pl.ds(f, RADIX, stride=8), :] for part in range(2)]
                columns.append(jnp.concatenate(parts, axis=0))
            values = jnp.concatenate(columns, axis=1).astype(BF16)
            mid = jnp.dot(tables[:256, :], values, preferred_element_type=F32)
            rows = []
            for s in range(2):
                re = mid[:RADIX, s * RADIX : (s + 1) * RADIX]
                im = mid[RADIX:, s * RADIX : (s + 1) * RADIX]
                rows.append(jnp.concatenate([re * tw_re - im * tw_im, re * tw_im + im * tw_re], axis=1).astype(BF16))
            rotated = jnp.concatenate(rows, axis=0)
            out = lax.dot_general(lhs[...], rotated, BOTH_LAST, preferred_element_type=F32)
            for part in range(2):
                for h in range(2):
                    for s in range(2):
                        at = part * RADIX + h * 64
                        columns = out[at : at + 64, s * RADIX : (s + 1) * RADIX]
                        turned[s * 4 + part * 2 + h, pl.ds(f, 64, stride=8), :] = columns
        for block in range(8):
            at = start * 512 + block * RADIX
            out_ref[:, :, at : at + RADIX] = turned[block].reshape(32, 16, RADIX).astype(BF16)


ANY = pl.BlockSpec(memory_space=pl.ANY)
VMEM = pl.BlockSpec(memory_space=pltpu.VMEM)
SMEM = pl.BlockSpec(memory_space=pltpu.SMEM)
GRANT = pltpu.CompilerParams(vmem_limit_bytes=56 * 2**20)
BRIEF = pl.CostEstimate(flops=1, bytes_accessed=1, transcendentals=0)


BOTH_LAST = (((1,), (1,)), ((), ()))


def channelize(voltages, filter_taps, band_order):
    tables, tw = constants(filter_taps.shape[1])
    return pl.pallas_call(
        channel_kernel,
        out_shape=jax.ShapeDtypeStruct((32, 16, 2048), BF16),
        in_specs=[VMEM] + [ANY] * 4,
        out_specs=VMEM,
        scratch_shapes=[
            pltpu.VMEM((2, 2, 8 * RADIX, RADIX), F32),
            pltpu.VMEM((8, 512, RADIX), F32),
            pltpu.VMEM((256, 256), BF16),
            pltpu.VMEM(tables.shape, BF16),
            pltpu.VMEM(tw.shape, F32),
            pltpu.VMEM(filter_taps.shape, F32),
            pltpu.VMEM(voltages.shape, BF16),
            pltpu.SemaphoreType.DMA((5,)),
        ],
        compiler_params=GRANT,
        cost_estimate=BRIEF,
        name="channelize",
    )(band_order.reshape(1, 64), tables, tw, filter_taps, voltages)


def times(gain, values):
    parts = []
    for at in range(0, values.shape[-1], 512):
        re, im = values[:, at : at + 256], values[:, at + 256 : at + 512]
        parts += [gain[0] * re - gain[1] * im, gain[0] * im + gain[1] * re]
    return jnp.concatenate(parts, axis=1)


def calibrate_kernel(at_ref, got_ref, gain_ref, up_ref, down_ref):
    half, low_band = at_ref[0], at_ref[1] < 2
    got = got_ref[...].astype(F32)
    swapped = half == 1
    own = jnp.where(swapped, got[:, 8:], got[:, :8]).reshape(256, got.shape[2])
    other = jnp.where(swapped, got[:, :8], got[:, 8:]).reshape(256, got.shape[2])
    own = times(gain_ref[:, :, half].astype(F32).reshape(2, 256, 256), own)
    up_ref[...] = jnp.where(low_band, own, other).astype(BF16)
    down_ref[...] = jnp.where(low_band, other, own).astype(BF16)


def calibrate(section, place, got, gains):
    return pl.pallas_call(
        calibrate_kernel,
        out_shape=[jax.ShapeDtypeStruct((256, 1024), BF16)] * 2,
        grid=(1,),
        in_specs=[
            SMEM,
            pl.BlockSpec((32, 16, 1024), lambda i: (0, 0, section)),
            pl.BlockSpec((2, 16, 2, 16, 256), lambda i: (0, 0, 0, 0, 0)),
        ],
        out_specs=[pl.BlockSpec((256, 1024), lambda i: (0, 0))] * 2,
        compiler_params=GRANT,
        cost_estimate=BRIEF,
        name="calibrate",
    )(place, got, gains)


def enter_kernel(at_ref, part_hbm, gain_hbm, out_hbm, part, gain, sems):
    @pl.when(at_ref[0] == 1)
    def _():
        loads = [pltpu.make_async_copy(part_hbm, part, sems.at[0]), pltpu.make_async_copy(gain_hbm, gain, sems.at[1])]
        for copy in loads:
            copy.start()
        for copy in loads:
            copy.wait()
        part[...] = times(gain[...].astype(F32).reshape(2, 256, 256), part[...].astype(F32)).astype(BF16)
        store = pltpu.make_async_copy(part, out_hbm, sems.at[2])
        store.start()
        store.wait()


def enter(is_entry, part, gain):
    return pl.pallas_call(
        enter_kernel,
        out_shape=jax.ShapeDtypeStruct(part.shape, BF16),
        in_specs=[SMEM, ANY, ANY],
        out_specs=ANY,
        scratch_shapes=[
            pltpu.VMEM(part.shape, BF16),
            pltpu.VMEM(gain.shape, BF16),
            pltpu.SemaphoreType.DMA((3,)),
        ],
        input_output_aliases={1: 0},
        compiler_params=GRANT,
        cost_estimate=BRIEF,
        name="enter",
    )(is_entry.astype(jnp.int32).reshape(1), part, gain)


def spread(mask, group):
    tile = lax.broadcasted_iota(jnp.int32, (64, 512), 0)
    column = lax.broadcasted_iota(jnp.int32, (64, 512), 1) // TILE + group * 16
    return jnp.dot(mask, (tile == column).astype(BF16), preferred_element_type=F32).astype(BF16)


def crossed(left):
    parts = []
    for at in range(0, left.shape[1], 512):
        parts += [left[:, at + 256 : at + 512], -left[:, at : at + 256]]
    return jnp.concatenate(parts, axis=1)


def fetch(low, half, sources, to, sems):
    waits = []
    for index, (below, above) in enumerate(sources):
        place = to.at[:, half if index == 0 else 1 - half]
        copies = [pltpu.make_async_copy(ref, place, sems.at[index]) for ref in (below, above)]
        pl.when(low)(copies[0].start)
        pl.when(jnp.logical_not(low))(copies[1].start)
        waits.append(copies[0])
    return waits


def weighted(mask, group, weight_ref, values):
    wide = spread(mask, group)
    both = jnp.concatenate([weight_ref[0] * wide, weight_ref[1] * wide], axis=0)
    total = jnp.dot(both, values, preferred_element_type=F32)
    parts = []
    for at in range(0, values.shape[1], 512):
        re, im = slice(at, at + 256), slice(at + 256, at + 512)
        parts += [total[:256, re] - total[256:, im], total[:256, im] + total[256:, re]]
    return jnp.concatenate(parts, axis=1)


def gather(half, band, sources, to, sems):
    low = band < 2
    same, swap = half, 1 - half
    up_0, down_0, up_1, down_1, up_2, down_2, up_3, down_3, up_4, down_4 = sources
    table = (
        (up_0, down_0, ((0, same), (1, same), (2, same), (3, same))),
        (up_1, up_1, ((3, swap), (0, same), (1, same), (2, swap))),
        (down_1, down_1, ((1, swap), (2, same), (3, same), (0, swap))),
        (up_2, up_2, ((2, swap), (3, swap), (0, same), (1, same))),
        (down_2, down_2, ((2, same), (3, same), (0, swap), (1, swap))),
        (up_3, up_3, ((1, same), (2, swap), (3, swap), (0, same))),
        (down_3, down_3, ((3, same), (0, swap), (1, swap), (2, same))),
        (down_4, up_4, ((0, swap), (1, swap), (2, swap), (3, swap))),
    )
    table = (table[0], table[7]) + table[1:7]
    for below, above, places in table:
        group = by_band(band, [g for g, _ in places])
        run = by_band(band, [r for _, r in places])
        sem = sems.at[group * 2 + run]
        copies = [pltpu.make_async_copy(ref, to.at[group, :, run], sem) for ref in (below, above)]
        pl.when(low)(copies[0].start)
        pl.when(jnp.logical_not(low))(copies[1].start)


def outer_band(band):
    return jnp.where(band < 2, 0, 3)


def share_kernel(at_ref, mask_ref, near_hbm, far_hbm, local_hbm, *refs):
    sources, (out_ref, held, weights, sems, weight_sems) = refs[:12], refs[-5:]
    half, band = at_ref[0], at_ref[1]
    low = band < 2
    rows = pl.ds(pl.multiple_of(outer_band(band) * 256, 256), 256)
    loads = [
        pltpu.make_async_copy(ref, weights.at[index], weight_sems.at[index])
        for index, ref in enumerate((near_hbm, far_hbm, local_hbm.at[:, rows, :]))
    ]
    for copy in loads:
        copy.start()
    for index in range(3):
        at = index * 4
        loads += fetch(low, half, (sources[at : at + 2], sources[at + 2 : at + 4]), held.at[index], sems.at[index])
    mask = mask_ref[...].astype(F32).astype(BF16)
    total = None
    for index, group in enumerate((jnp.where(low, 2, 1), jnp.where(low, 3, 0), band)):
        for copy in (loads[index], loads[3 + 2 * index], loads[4 + 2 * index]):
            copy.wait()
        now = weighted(mask, group, weights.at[index], held[index].reshape(512, 1024))
        total = now if total is None else total + now
    out_ref[...] = total.astype(BF16)


def outer_share(place, mask, near, far, local, up, down):
    sources = (down[1], up[1], up[3], down[3], down[2], up[2], up[2], down[2], up[0], down[0], down[4], up[4])
    return pl.pallas_call(
        share_kernel,
        out_shape=jax.ShapeDtypeStruct((256, 1024), BF16),
        grid_spec=pltpu.PrefetchScalarGridSpec(
            num_scalar_prefetch=1,
            grid=(1,),
            in_specs=[pl.BlockSpec((256, 64), lambda i, at: (outer_band(at[1]), 0))] + [ANY] * 15,
            out_specs=pl.BlockSpec((256, 1024), lambda i, at: (0, 0)),
            scratch_shapes=[
                pltpu.VMEM((3, 16, 2, 16, 1024), BF16),
                pltpu.VMEM((3, 2, 256, 512), BF16),
                pltpu.SemaphoreType.DMA((3, 2)),
                pltpu.SemaphoreType.DMA((3,)),
            ],
        ),
        compiler_params=GRANT,
        cost_estimate=BRIEF,
        name="outer_share",
    )(place, mask, near, far, local, *[part.reshape(16, 16, 1024) for part in sources])


def edge_kernel(average, at_ref, *refs):
    sources, (block_ref, far, own, sems) = refs[:16], refs[-4:]
    half, low = at_ref[0], at_ref[1] < 2
    waits = []
    for section in range(2):
        parts = sources[section * 8 : section * 8 + 8]
        waits.append(
            fetch(low, half, (parts[0:2], parts[2:4]), far.at[section], sems.at[section, 0])
            + fetch(low, half, (parts[4:6], parts[6:8]), own.at[section], sems.at[section, 1])
        )
    total = None
    for section in range(2):
        for copy in waits[section]:
            copy.wait()
        left, right = own[section].reshape(512, 1024), far[section].reshape(512, 1024)
        both = jnp.concatenate([left, crossed(left)], axis=0)
        now = lax.dot_general(both, right, BOTH_LAST, preferred_element_type=F32)
        total = now if total is None else total + now
    block_ref[0] = (total[:512] * average).astype(BF16)
    block_ref[1] = (total[512:] * average).astype(BF16)


def edge(average, place, ups, downs, *after):
    parts = []
    for up, down in zip(ups, downs):
        parts += [up[1], down[1], down[3], up[3], up[0], down[0], down[4], up[4]]
    return pl.pallas_call(
        lambda *refs: edge_kernel(average, *refs),
        out_shape=jax.ShapeDtypeStruct((2, 512, 512), BF16),
        in_specs=[SMEM] + [ANY] * (16 + len(after)),
        out_specs=VMEM,
        scratch_shapes=[pltpu.VMEM((2, 16, 2, 16, 1024), BF16)] * 2 + [pltpu.SemaphoreType.DMA((2, 2, 2))],
        compiler_params=GRANT,
        cost_estimate=BRIEF,
        name="edge",
    )(place, *[part.reshape(16, 16, 1024) for part in parts], *after)


def pair_kernel(average, at_ref, *refs):
    sources, block_hbm, (out_ref, section_a, section_b, held, lhs, made, sems, out_sems) = refs[:20], refs[20], refs[-8:]
    half, band = at_ref[0], at_ref[1]
    partner = band ^ 1
    inner = (band == 1) | (band == 2)
    load = pltpu.make_async_copy(block_hbm, made.at[3], out_sems.at[5])
    load.start()
    for index in range(2):
        gather(half, band, sources[index * 10 : (index + 1) * 10], held.at[index], sems.at[index])

    def arrived(index, group):
        for run in range(2):
            pltpu.make_async_copy(sources[0], held.at[index, group, :, run], sems.at[index, group * 2 + run]).wait()

    for index in range(2):
        arrived(index, band)
        left = held[index, band].reshape(512, 1024)
        lhs[:512, index * 1024 : (index + 1) * 1024] = left
        lhs[512:, index * 1024 : (index + 1) * 1024] = crossed(left)

    def columns(step, group):
        total = None
        for index in range(2):
            right = held[index, group].reshape(512, 1024)
            now = lax.dot_general(
                lhs[:, index * 1024 : (index + 1) * 1024], right, BOTH_LAST, preferred_element_type=F32
            )
            total = now if total is None else total + now
        made[step, 0] = (total[:512] * average).astype(BF16)
        made[step, 1] = (total[512:] * average).astype(BF16)
        lanes = pl.ds(pl.multiple_of(group * 512, 512), 512)
        store = pltpu.make_async_copy(made.at[step], out_ref.at[:, :, lanes], out_sems.at[2 + step])
        store.start()
        return store

    stores = [columns(0, band)]
    for group in (band ^ 2, band ^ 3, partner):
        for index in range(2):
            arrived(index, group)
    kept = [pltpu.make_async_copy(held.at[i], to, out_sems.at[i]) for i, to in enumerate((section_a, section_b))]
    for copy in kept:
        copy.start()
    stores += [columns(1, band ^ 2), columns(2, band ^ 3)]
    load.wait()

    @pl.when(inner)
    def _():
        lanes = pl.ds(pl.multiple_of(partner * 512, 512), 512)
        store = pltpu.make_async_copy(made.at[3], out_ref.at[:, :, lanes], out_sems.at[5])
        store.start()
        store.wait()

    for copy in kept + stores:
        copy.wait()


def pairs(average, place, ups, downs, block, *after):
    parts = []
    for up, down in zip(ups, downs):
        parts += [part.reshape(16, 16, 1024) for pair in zip(up, down) for part in pair]
    section = jax.ShapeDtypeStruct((4, 16, 2, 16, 1024), BF16)
    visibility, *sections = pl.pallas_call(
        lambda *refs: pair_kernel(average, *refs),
        out_shape=[jax.ShapeDtypeStruct((2, 512, 2048), BF16), section, section],
        in_specs=[SMEM] + [ANY] * (21 + len(after)),
        out_specs=[ANY] * 3,
        scratch_shapes=[
            pltpu.VMEM((2, 4, 16, 2, 16, 1024), BF16),
            pltpu.VMEM((1024, 2048), BF16),
            pltpu.VMEM((4, 2, 512, 512), BF16),
            pltpu.SemaphoreType.DMA((2, 8)),
            pltpu.SemaphoreType.DMA((6,)),
        ],
        compiler_params=GRANT,
        cost_estimate=BRIEF,
        name="pairs",
    )(place, *parts, block, *after)
    return visibility, [section.reshape(2048, 1024) for section in sections]


def last_kernel(at_ref, block_hbm, whole_hbm, out_hbm, block, turned, sem):
    band = at_ref[1]

    @pl.when((band == 0) | (band == 3))
    def _():
        lanes = pl.ds(pl.multiple_of((band ^ 1) * 512, 512), 512)
        load = pltpu.make_async_copy(block_hbm, block, sem)
        load.start()
        load.wait()
        turned[0] = block[0].astype(F32).T.astype(BF16)
        turned[1] = (-block[1].astype(F32).T).astype(BF16)
        store = pltpu.make_async_copy(turned, out_hbm.at[:, :, lanes], sem)
        store.start()
        store.wait()


def last_pairs(place, block, visibility):
    return pl.pallas_call(
        last_kernel,
        out_shape=jax.ShapeDtypeStruct((2, 512, 2048), BF16),
        in_specs=[SMEM, ANY, ANY],
        out_specs=ANY,
        scratch_shapes=[pltpu.VMEM((2, 512, 512), BF16)] * 2 + [pltpu.SemaphoreType.DMA],
        input_output_aliases={2: 0},
        compiler_params=GRANT,
        cost_estimate=BRIEF,
        name="last_pairs",
    )(place, block, visibility)


def beam_kernel(at_ref, mask_ref, local_ref, near_ref, far_ref, end_ref, section_a, section_b, out_ref, weights):
    step, band = pl.program_id(0), at_ref[1]
    low = band < 2

    @pl.when(step == 0)
    def _():
        mask = mask_ref[...].astype(F32).astype(BF16)
        pieces = (
            (band, local_ref),
            (jnp.where(low, 2, 1), near_ref),
            (jnp.where(low, 3, 0), far_ref),
            (jnp.where(low, 1 - band, 5 - band), end_ref),
        )
        for group, piece_ref in pieces:
            lanes = pl.ds(pl.multiple_of(group * 512, 512), 512)
            wide = spread(mask, group)
            for part in range(2):
                weights[part * 256 : (part + 1) * 256, lanes] = piece_ref[part] * wide

    def form(section_ref):
        total = jnp.dot(weights[...], section_ref[...], preferred_element_type=F32)
        out_ref[:, :256] = total[:256, :256] - total[256:, 256:]
        out_ref[:, 256:] = total[:256, 256:] + total[256:, :256]

    pl.when(step < 2)(lambda: form(section_a))
    pl.when(step >= 2)(lambda: form(section_b))


def beams(place, mask, local, others, sections):
    return pl.pallas_call(
        beam_kernel,
        out_shape=jax.ShapeDtypeStruct((256, 2048), F32),
        grid_spec=pltpu.PrefetchScalarGridSpec(
            num_scalar_prefetch=1,
            grid=(4,),
            in_specs=[
                pl.BlockSpec((256, 64), lambda i, at: (at[1], 0)),
                pl.BlockSpec((2, 256, 512), lambda i, at: (0, at[1], 0)),
            ]
            + [pl.BlockSpec((2, 256, 512), lambda i, at: (0, 0, 0))] * 3
            + [
                pl.BlockSpec((2048, 512), lambda i, at: (0, jnp.minimum(i, 1))),
                pl.BlockSpec((2048, 512), lambda i, at: (0, jnp.maximum(i - 2, 0))),
            ],
            out_specs=pl.BlockSpec((256, 512), lambda i, at: (0, i)),
            scratch_shapes=[pltpu.VMEM((512, 2048), BF16)],
        ),
        compiler_params=GRANT,
        cost_estimate=BRIEF,
        name="beams",
    )(place, mask, local, *others, *sections)


def finish_kernel(at_ref, formed_ref, share_a, share_b, *refs):
    out_ref, turned = refs[-2:]
    is_outer = (at_ref[1] == 0) | (at_ref[1] == 3)
    for spectrum in range(4):
        share_ref = (share_a, share_b)[spectrum // 2]
        for part in range(2):
            at = spectrum * 512 + part * 256
            total = formed_ref[:, at : at + 256]
            at = at % 1024
            total = total + jnp.where(is_outer, share_ref[:, at : at + 256].astype(F32), 0.0)
            for lane in range(2):
                turned[lane, pl.ds(part * 4 + spectrum, 256, stride=8), :] = total[:, lane * 128 : (lane + 1) * 128]
    for lane in range(2):
        out_ref[:, :, lane * 128 : (lane + 1) * 128] = turned[lane].reshape(512, 4, 128).astype(BF16)


def finish(place, formed, shares, *after):
    return pl.pallas_call(
        finish_kernel,
        out_shape=jax.ShapeDtypeStruct((512, 4, 256), BF16),
        in_specs=[SMEM] + [VMEM] * 3 + [ANY] * len(after),
        out_specs=VMEM,
        scratch_shapes=[pltpu.VMEM((2, 2048, 128), F32)],
        compiler_params=GRANT,
        cost_estimate=BRIEF,
        name="finish",
    )(place, formed, *shares, *after)


def by_band(band, values):
    first, second, third, fourth = values
    return jnp.where(band < 2, jnp.where(band == 0, first, second), jnp.where(band == 2, third, fourth))


def shards(voltages, filter_taps, feed_gains, beam_weights, beam_mask, band_order):
    feed, band = lax.axis_index("feed"), lax.axis_index("band")
    half = lax.shift_right_logical(feed, 1) & 1
    low = band < 2
    everyone = (0, 1, 2, 3)
    place = jnp.stack([half, band])

    gains = feed_gains.reshape(2, 16, 2, 16, 256)
    sent_gain = lax.dynamic_index_in_dim(gains, 1 - half, 2, keepdims=False)
    entry_gains = (
        lax.ppermute(sent_gain, BOTH, hop(-3, (3,)) + hop(3, (0,))),
        lax.ppermute(sent_gain, BOTH, hop(-2, (2,)) + hop(2, (1,))),
    )
    own_weights = beam_weights[:, 0]
    from_near, from_far, from_end = hop(1, (1,)) + hop(-1, (2,)), hop(2, (0,)) + hop(-2, (3,)), hop(1, (0,)) + hop(-1, (3,))
    away = lax.dynamic_slice_in_dim(own_weights, jnp.where(low, 768, 0), 256, 1)
    near_outer = lax.ppermute(away, BOTH, from_near)
    far_outer = lax.ppermute(away, BOTH, from_far)

    spectra = channelize(voltages, filter_taps, band_order)
    got = lax.all_to_all(spectra, "feed", 0, 0, axis_index_groups=PLANE_GROUPS, tiled=True)
    got, near_outer, *entry_gains = lax.optimization_barrier((got, near_outer) + entry_gains)
    entry_gains[1], far_outer = lax.optimization_barrier((entry_gains[1], far_outer))
    ups, downs = [], []
    for section in range(2):
        up, down = ([part] for part in calibrate(section, place, got, gains))
        for step, senders in enumerate((everyone, everyone, (0, 1, 2), (1, 2))):
            up.append(lax.ppermute(up[-1], BOTH, hop(1, senders)))
            down.append(lax.ppermute(down[-1], BOTH, hop(-1, tuple(3 - p for p in senders))))
            if step < 2:
                up[-1] = enter(band == 0, up[-1], entry_gains[step])
                down[-1] = enter(band == 3, down[-1], entry_gains[step])
        ups.append(up)
        downs.append(down)

    average = 1.0 / 1024
    inward = hop(-1, (1,)) + hop(1, (2,))
    shares = []
    for up, down in zip(ups, downs):
        shares.append(outer_share(place, beam_mask, near_outer, far_outer, own_weights, up, down))
        if len(shares) == 1:
            block = edge(average, place, ups, downs, shares[0])
    shares[1], _ = lax.optimization_barrier((shares[1], block))
    received = lax.ppermute(block, BOTH, inward)
    shares = [lax.ppermute(share, BOTH, inward) for share in shares]

    late, _, _ = lax.optimization_barrier((own_weights, block, shares[0]))
    away = lax.dynamic_slice_in_dim(late, jnp.where(low, 512, 256), 256, 1)
    near = lax.ppermute(away, BOTH, from_near)
    far = lax.ppermute(away, BOTH, from_far)
    away = lax.dynamic_slice_in_dim(late, jnp.where(low, 256, 512), 256, 1)
    end = lax.ppermute(away, BOTH, from_end)

    visibility, sections = pairs(average, place, ups, downs, block, shares[0])
    visibility = last_pairs(place, received, visibility)
    formed = finish(place, beams(place, beam_mask, own_weights, (near, far, end), sections), shares, visibility)
    return (visibility[:, None], formed.reshape(1, 256, 2, 4, 256))


def solution(mesh):
    return jax.shard_map(
        shards,
        mesh=mesh,
        in_specs=(
            P(None, ("band", "feed"), None),
            P(),
            P(None, "feed", "band", None),
            P(None, "feed", None, "band"),
            P(),
            P(),
        ),
        out_specs=(P(None, "feed", "band", None), P("feed", "band", None, None, None)),
        check_vma=False,
    )
```

```python
import math

import jax
import jax.numpy as jnp
import numpy as np
from jax import lax
from jax.experimental import pallas as pl
from jax.experimental.pallas import tpu as pltpu
from jax.sharding import PartitionSpec as P

RADIX = 128
TILE = 32
SIDE = 4
BOTH = ("feed", "band")
F32 = jnp.float32
BF16 = jnp.bfloat16


def feed_at(y, x, half, core):
    return ((y * SIDE + x) * 2 + half) * 2 + core


PLANE_GROUPS = [
    [feed_at(y, x, half, core) for y in range(SIDE) for x in range(SIDE) for core in range(2)]
    for half in range(2)
]


def hop(step, senders):
    pairs = []
    for y in range(SIDE):
        for x in range(SIDE):
            for core in range(2):
                for z in range(8):
                    if z % 4 in senders:
                        to = (z + step) % 8
                        pairs.append(
                            (feed_at(y, x, z // 4, core) * 4 + z % 4, feed_at(y, x, to // 4, core) * 4 + to % 4)
                        )
    return pairs


def constants(length):
    row = np.arange(RADIX)
    angles = (row[:, None] * row[None, :] % RADIX) * (2.0 * math.pi / RADIX)
    factor = 1.0 / math.sqrt(RADIX)
    re = (np.cos(angles) * factor).astype(np.float32)
    im = (-np.sin(angles) * factor).astype(np.float32)
    first = np.block([[re, -im], [im, re]])
    second = np.stack([np.hstack([re, -im]), np.hstack([im, re])])
    second = second.reshape(2, RADIX // 2, 2, 2 * RADIX).transpose(0, 2, 1, 3).reshape(2 * RADIX, 2 * RADIX)
    twiddle = (row[:, None] * row[None, :] % length) * (2.0 * math.pi / length)
    tw = np.stack([np.cos(twiddle), -np.sin(twiddle)]).astype(np.float32)
    place = np.zeros((64, 2 * RADIX), np.float32)
    for yx in range(16):
        for core in range(2):
            for half in range(2):
                place[(yx * 2 + core) * 2 + half, (yx * 2 + half) * 2 + core] = 1.0
    return (jnp.asarray(np.concatenate([first, second, place]), BF16), jnp.asarray(tw))


def channel_kernel(order_ref, tables_hbm, tw_hbm, taps_hbm, volts_hbm, out_ref, frame, turned, lhs, tables, tw_ref, taps_ref, volts_ref, sems):
    length = taps_ref.shape[1]
    early, late = pl.ds(0, 5 * length), pl.ds(5 * length, 2 * length)
    copies = [
        pltpu.make_async_copy(tables_hbm, tables, sems.at[0]),
        pltpu.make_async_copy(taps_hbm, taps_ref, sems.at[1]),
        pltpu.make_async_copy(volts_hbm.at[:, :, early], volts_ref.at[:, :, early], sems.at[2]),
        pltpu.make_async_copy(tw_hbm, tw_ref, sems.at[3]),
        pltpu.make_async_copy(volts_hbm.at[:, :, late], volts_ref.at[:, :, late], sems.at[4]),
    ]
    for copy in copies:
        copy.start()
    pick = (order_ref[...] == lax.broadcasted_iota(jnp.int32, (64, 64), 0)).astype(BF16)
    copies[0].wait()
    pick = lax.dot_general(tables[512:576, :64], pick, BOTH_LAST, preferred_element_type=F32).astype(BF16)
    for part in range(4):
        second = tables[256 + part * 64 : 256 + (part + 1) * 64, :]
        lhs[part * 64 : (part + 1) * 64, :] = jnp.dot(pick, second, preferred_element_type=F32).astype(BF16)
    width = 16 * RADIX
    for copy in copies[1:4]:
        copy.wait()
    for start in (0, 2):
        if start:
            copies[4].wait()

        def filter_chunk(chunk, carry):
            lane = pl.multiple_of(chunk * width, width)
            taps = [jnp.broadcast_to(taps_ref[t : t + 1, pl.ds(lane, width)], (8, width)) for t in range(4)]
            for part in range(2):
                volts = [volts_ref[part, :, pl.ds((start + n) * length + lane, width)].astype(F32) for n in range(5)]
                for s in range(2):
                    total = taps[0] * volts[s]
                    for t in range(1, 4):
                        total = total + taps[t] * volts[s + t]
                    for a in range(16):
                        at = pl.multiple_of(chunk * width // RADIX * 8 + a * 8, 8)
                        frame[s, part, pl.ds(at, 8), :] = total[:, a * RADIX : (a + 1) * RADIX]
            return carry

        lax.fori_loop(0, length // width, filter_chunk, 0)
        tw_re, tw_im = tw_ref[0], tw_ref[1]
        for f in range(8):
            columns = []
            for s in range(2):
                parts = [frame[s, part, pl.ds(f, RADIX, stride=8), :] for part in range(2)]
                columns.append(jnp.concatenate(parts, axis=0))
            values = jnp.concatenate(columns, axis=1).astype(BF16)
            mid = jnp.dot(tables[:256, :], values, preferred_element_type=F32)
            rows = []
            for s in range(2):
                re = mid[:RADIX, s * RADIX : (s + 1) * RADIX]
                im = mid[RADIX:, s * RADIX : (s + 1) * RADIX]
                rows.append(jnp.concatenate([re * tw_re - im * tw_im, re * tw_im + im * tw_re], axis=1).astype(BF16))
            rotated = jnp.concatenate(rows, axis=0)
            out = lax.dot_general(lhs[...], rotated, BOTH_LAST, preferred_element_type=F32)
            for part in range(2):
                for h in range(2):
                    for s in range(2):
                        at = part * RADIX + h * 64
                        columns = out[at : at + 64, s * RADIX : (s + 1) * RADIX]
                        turned[s * 4 + part * 2 + h, pl.ds(f, 64, stride=8), :] = columns
        for block in range(8):
            at = start * 512 + block * RADIX
            out_ref[:, :, at : at + RADIX] = turned[block].reshape(32, 16, RADIX).astype(BF16)


ANY = pl.BlockSpec(memory_space=pltpu.HBM)
VMEM = pl.BlockSpec(memory_space=pltpu.VMEM)
SMEM = pl.BlockSpec(memory_space=pltpu.SMEM)
GRANT = pltpu.CompilerParams(vmem_limit_bytes=63 * 2**20 + 2**19)
BRIEF = pl.CostEstimate(flops=1, bytes_accessed=1, transcendentals=0)


BOTH_LAST = (((1,), (1,)), ((), ()))


def channelize(voltages, filter_taps, band_order):
    tables, tw = constants(filter_taps.shape[1])
    return pl.pallas_call(
        channel_kernel,
        out_shape=jax.ShapeDtypeStruct((32, 16, 2048), BF16),
        in_specs=[VMEM] + [ANY] * 4,
        out_specs=VMEM,
        scratch_shapes=[
            pltpu.VMEM((2, 2, 8 * RADIX, RADIX), F32),
            pltpu.VMEM((8, 512, RADIX), F32),
            pltpu.VMEM((256, 256), BF16),
            pltpu.VMEM(tables.shape, BF16),
            pltpu.VMEM(tw.shape, F32),
            pltpu.VMEM(filter_taps.shape, F32),
            pltpu.VMEM(voltages.shape, BF16),
            pltpu.SemaphoreType.DMA((5,)),
        ],
        compiler_params=GRANT,
        cost_estimate=BRIEF,
        name="channelize",
    )(band_order.reshape(1, 64), tables, tw, filter_taps, voltages)


def times(gain, values):
    parts = []
    for at in range(0, values.shape[-1], 512):
        re, im = values[:, at : at + 256], values[:, at + 256 : at + 512]
        parts += [gain[0] * re - gain[1] * im, gain[0] * im + gain[1] * re]
    return jnp.concatenate(parts, axis=1)


def calibrate_kernel(section, at_ref, got_hbm, gain_hbm, up_ref, down_ref, got_ref, gain_ref, sems):
    half, low_band = at_ref[0], at_ref[1] < 2
    loads = [
        pltpu.make_async_copy(got_hbm.at[:, :, pl.ds(section * 1024, 1024)], got_ref, sems.at[0]),
        pltpu.make_async_copy(gain_hbm.at[:, :, half], gain_ref, sems.at[1]),
    ]
    for copy in loads:
        copy.start()
    for copy in loads:
        copy.wait()
    got = got_ref[...].astype(F32)
    swapped = half == 1
    own = jnp.where(swapped, got[:, 8:], got[:, :8]).reshape(256, got.shape[2])
    other = jnp.where(swapped, got[:, :8], got[:, 8:]).reshape(256, got.shape[2])
    own = times(gain_ref[...].astype(F32).reshape(2, 256, 256), own)
    up_ref[...] = jnp.where(low_band, own, other).astype(BF16)
    down_ref[...] = jnp.where(low_band, other, own).astype(BF16)


def calibrate(section, place, got, gains):
    return pl.pallas_call(
        lambda *refs: calibrate_kernel(section, *refs),
        out_shape=[jax.ShapeDtypeStruct((256, 1024), BF16)] * 2,
        in_specs=[SMEM, ANY, ANY],
        out_specs=[VMEM] * 2,
        scratch_shapes=[
            pltpu.VMEM((32, 16, 1024), BF16),
            pltpu.VMEM((2, 16, 16, 256), BF16),
            pltpu.SemaphoreType.DMA((2,)),
        ],
        compiler_params=GRANT,
        cost_estimate=BRIEF,
        name="calibrate",
    )(place, got, gains)


def enter_kernel(at_ref, part_hbm, gain_hbm, out_hbm, part, gain, sems):
    @pl.when(at_ref[0] == 1)
    def _():
        loads = [pltpu.make_async_copy(part_hbm, part, sems.at[0]), pltpu.make_async_copy(gain_hbm, gain, sems.at[1])]
        for copy in loads:
            copy.start()
        for copy in loads:
            copy.wait()
        part[...] = times(gain[...].astype(F32).reshape(2, 256, 256), part[...].astype(F32)).astype(BF16)
        store = pltpu.make_async_copy(part, out_hbm, sems.at[2])
        store.start()
        store.wait()


def enter(is_entry, part, gain):
    return pl.pallas_call(
        enter_kernel,
        out_shape=jax.ShapeDtypeStruct(part.shape, BF16),
        in_specs=[SMEM, ANY, ANY],
        out_specs=ANY,
        scratch_shapes=[
            pltpu.VMEM(part.shape, BF16),
            pltpu.VMEM(gain.shape, BF16),
            pltpu.SemaphoreType.DMA((3,)),
        ],
        input_output_aliases={1: 0},
        compiler_params=GRANT,
        cost_estimate=BRIEF,
        name="enter",
    )(is_entry.astype(jnp.int32).reshape(1), part, gain)


def spread(mask, group):
    tile = lax.broadcasted_iota(jnp.int32, (64, 512), 0)
    column = lax.broadcasted_iota(jnp.int32, (64, 512), 1) // TILE + group * 16
    return jnp.dot(mask, (tile == column).astype(BF16), preferred_element_type=F32).astype(BF16)


def crossed(left):
    parts = []
    for at in range(0, left.shape[1], 512):
        parts += [left[:, at + 256 : at + 512], -left[:, at : at + 256]]
    return jnp.concatenate(parts, axis=1)


def fetch(low, half, sources, to, sems):
    waits = []
    for index, (below, above) in enumerate(sources):
        place = to.at[:, half if index == 0 else 1 - half]
        copies = [pltpu.make_async_copy(ref, place, sems.at[index]) for ref in (below, above)]
        pl.when(low)(copies[0].start)
        pl.when(jnp.logical_not(low))(copies[1].start)
        waits.append(copies[0])
    return waits


def weighted(mask, group, weight_ref, values):
    wide = spread(mask, group)
    both = jnp.concatenate([weight_ref[0] * wide, weight_ref[1] * wide], axis=0)
    total = jnp.dot(both, values, preferred_element_type=F32)
    parts = []
    for at in range(0, values.shape[1], 512):
        re, im = slice(at, at + 256), slice(at + 256, at + 512)
        parts += [total[:256, re] - total[256:, im], total[:256, im] + total[256:, re]]
    return jnp.concatenate(parts, axis=1)


def gather(half, band, sources, to, sems):
    low = band < 2
    same, swap = half, 1 - half
    up_0, down_0, up_1, down_1, up_2, down_2, up_3, down_3, up_4, down_4 = sources
    table = (
        (up_0, down_0, ((0, same), (1, same), (2, same), (3, same))),
        (up_1, up_1, ((3, swap), (0, same), (1, same), (2, swap))),
        (down_1, down_1, ((1, swap), (2, same), (3, same), (0, swap))),
        (up_2, up_2, ((2, swap), (3, swap), (0, same), (1, same))),
        (down_2, down_2, ((2, same), (3, same), (0, swap), (1, swap))),
        (up_3, up_3, ((1, same), (2, swap), (3, swap), (0, same))),
        (down_3, down_3, ((3, same), (0, swap), (1, swap), (2, same))),
        (down_4, up_4, ((0, swap), (1, swap), (2, swap), (3, swap))),
    )
    table = (table[0], table[7]) + table[1:7]
    for below, above, places in table:
        group = by_band(band, [g for g, _ in places])
        run = by_band(band, [r for _, r in places])
        sem = sems.at[group * 2 + run]
        copies = [pltpu.make_async_copy(ref, to.at[group, :, run], sem) for ref in (below, above)]
        pl.when(low)(copies[0].start)
        pl.when(jnp.logical_not(low))(copies[1].start)


def outer_band(band):
    return jnp.where(band < 2, 0, 3)


def share_kernel(give, at_ref, mask_ref, near_hbm, far_hbm, local_hbm, *refs):
    sources, (out_ref, held, weights, sems, weight_sems) = refs[:12], refs[-5:]
    half, band = at_ref[0], at_ref[1]
    low = band < 2
    inner = (band == 1) | (band == 2)

    def local(row):
        rows = pl.ds(pl.multiple_of(row, 256), 256)
        return pltpu.make_async_copy(local_hbm.at[:, rows, :], weights.at[2], weight_sems.at[2])

    @pl.when(inner)
    def _():
        loads = [
            pltpu.make_async_copy(near_hbm, weights.at[0], weight_sems.at[0]),
            pltpu.make_async_copy(far_hbm, weights.at[1], weight_sems.at[1]),
            local(outer_band(band) * 256),
        ]
        for copy in loads:
            copy.start()
        for index in range(3):
            at = index * 4
            loads += fetch(low, half, (sources[at : at + 2], sources[at + 2 : at + 4]), held.at[index], sems.at[index])
        mask = mask_ref[...].astype(F32).astype(BF16)
        total = None
        for index, group in enumerate((jnp.where(low, 2, 1), jnp.where(low, 3, 0), band)):
            for copy in (loads[index], loads[3 + 2 * index], loads[4 + 2 * index]):
                copy.wait()
            now = weighted(mask, group, weights.at[index], held[index].reshape(512, 1024))
            total = now if total is None else total + now
        out_ref[...] = total.astype(BF16)

    if give:

        @pl.when(jnp.logical_not(inner))
        def _():
            load = local(jnp.where(low, 256, 512))
            load.start()
            load.wait()
            for part in range(2):
                out_ref[:, part * 512 : (part + 1) * 512] = weights[2, part]


def outer_share(give, place, mask, near, far, local, up, down):
    sources = (down[1], up[1], up[3], down[3], down[2], up[2], up[2], down[2], up[0], down[0], down[4], up[4])
    return pl.pallas_call(
        lambda *refs: share_kernel(give, *refs),
        out_shape=jax.ShapeDtypeStruct((256, 1024), BF16),
        grid_spec=pltpu.PrefetchScalarGridSpec(
            num_scalar_prefetch=1,
            grid=(1,),
            in_specs=[pl.BlockSpec((256, 64), lambda i, at: (outer_band(at[1]), 0))] + [ANY] * 15,
            out_specs=pl.BlockSpec((256, 1024), lambda i, at: (0, 0)),
            scratch_shapes=[
                pltpu.VMEM((3, 16, 2, 16, 1024), BF16),
                pltpu.VMEM((3, 2, 256, 512), BF16),
                pltpu.SemaphoreType.DMA((3, 2)),
                pltpu.SemaphoreType.DMA((3,)),
            ],
        ),
        compiler_params=GRANT,
        cost_estimate=BRIEF,
        name="outer_share",
    )(place, mask, near, far, local, *[part.reshape(16, 16, 1024) for part in sources])


def edge_kernel(average, at_ref, *refs):
    sources, (block_ref, far, own, sems) = refs[:16], refs[-4:]
    half, band = at_ref[0], at_ref[1]
    low = band < 2

    @pl.when((band == 1) | (band == 2))
    def _():
        waits = []
        for section in range(2):
            parts = sources[section * 8 : section * 8 + 8]
            waits.append(
                fetch(low, half, (parts[0:2], parts[2:4]), far.at[section], sems.at[section, 0])
                + fetch(low, half, (parts[4:6], parts[6:8]), own.at[section], sems.at[section, 1])
            )
        total = None
        for section in range(2):
            for copy in waits[section]:
                copy.wait()
            left, right = own[section].reshape(512, 1024), far[section].reshape(512, 1024)
            both = jnp.concatenate([left, crossed(left)], axis=0)
            now = lax.dot_general(both, right, BOTH_LAST, preferred_element_type=F32)
            total = now if total is None else total + now
        block_ref[0] = (total[:512] * average).astype(BF16)
        block_ref[1] = (total[512:] * average).astype(BF16)


def edge(average, place, ups, downs, *after):
    parts = []
    for up, down in zip(ups, downs):
        parts += [up[1], down[1], down[3], up[3], up[0], down[0], down[4], up[4]]
    return pl.pallas_call(
        lambda *refs: edge_kernel(average, *refs),
        out_shape=jax.ShapeDtypeStruct((2, 512, 512), BF16),
        in_specs=[SMEM] + [ANY] * (16 + len(after)),
        out_specs=VMEM,
        scratch_shapes=[pltpu.VMEM((2, 16, 2, 16, 1024), BF16)] * 2 + [pltpu.SemaphoreType.DMA((2, 2, 2))],
        compiler_params=GRANT,
        cost_estimate=BRIEF,
        name="edge",
    )(place, *[part.reshape(16, 16, 1024) for part in parts], *after)


def pair_kernel(average, at_ref, *refs):
    sources, block_hbm, (out_ref, section_a, section_b, held, lhs, made, sems, out_sems) = refs[:20], refs[20], refs[-8:]
    half, band = at_ref[0], at_ref[1]
    partner = band ^ 1
    inner = (band == 1) | (band == 2)
    load = pltpu.make_async_copy(block_hbm, made.at[3], out_sems.at[5])
    load.start()
    for index in range(2):
        gather(half, band, sources[index * 10 : (index + 1) * 10], held.at[index], sems.at[index])

    def arrived(index, group):
        for run in range(2):
            pltpu.make_async_copy(sources[0], held.at[index, group, :, run], sems.at[index, group * 2 + run]).wait()

    for index in range(2):
        arrived(index, band)
        left = held[index, band].reshape(512, 1024)
        lhs[:512, index * 1024 : (index + 1) * 1024] = left
        lhs[512:, index * 1024 : (index + 1) * 1024] = crossed(left)

    def columns(step, group):
        total = None
        for index in range(2):
            right = held[index, group].reshape(512, 1024)
            now = lax.dot_general(
                lhs[:, index * 1024 : (index + 1) * 1024], right, BOTH_LAST, preferred_element_type=F32
            )
            total = now if total is None else total + now
        made[step, 0] = (total[:512] * average).astype(BF16)
        made[step, 1] = (total[512:] * average).astype(BF16)
        lanes = pl.ds(pl.multiple_of(group * 512, 512), 512)
        store = pltpu.make_async_copy(made.at[step], out_ref.at[:, :, lanes], out_sems.at[2 + step])
        store.start()
        return store

    stores = [columns(0, band)]
    for group in (band ^ 2, band ^ 3, partner):
        for index in range(2):
            arrived(index, group)
    kept = [pltpu.make_async_copy(held.at[i], to, out_sems.at[i]) for i, to in enumerate((section_a, section_b))]
    for copy in kept:
        copy.start()
    stores += [columns(1, band ^ 2), columns(2, band ^ 3)]
    load.wait()

    @pl.when(inner)
    def _():
        lanes = pl.ds(pl.multiple_of(partner * 512, 512), 512)
        store = pltpu.make_async_copy(made.at[3], out_ref.at[:, :, lanes], out_sems.at[5])
        store.start()
        store.wait()

    for copy in kept + stores:
        copy.wait()


def pairs(average, place, ups, downs, block, *after):
    parts = []
    for up, down in zip(ups, downs):
        parts += [part.reshape(16, 16, 1024) for pair in zip(up, down) for part in pair]
    section = jax.ShapeDtypeStruct((4, 16, 2, 16, 1024), BF16)
    visibility, *sections = pl.pallas_call(
        lambda *refs: pair_kernel(average, *refs),
        out_shape=[jax.ShapeDtypeStruct((2, 512, 2048), BF16), section, section],
        in_specs=[SMEM] + [ANY] * (21 + len(after)),
        out_specs=[ANY] * 3,
        scratch_shapes=[
            pltpu.VMEM((2, 4, 16, 2, 16, 1024), BF16),
            pltpu.VMEM((1024, 2048), BF16),
            pltpu.VMEM((4, 2, 512, 512), BF16),
            pltpu.SemaphoreType.DMA((2, 8)),
            pltpu.SemaphoreType.DMA((6,)),
        ],
        compiler_params=GRANT,
        cost_estimate=BRIEF,
        name="pairs",
    )(place, *parts, block, *after)
    return visibility, [section.reshape(2048, 1024) for section in sections]


def last_kernel(at_ref, block_hbm, whole_hbm, out_hbm, block, turned, sem):
    band = at_ref[1]

    @pl.when((band == 0) | (band == 3))
    def _():
        lanes = pl.ds(pl.multiple_of((band ^ 1) * 512, 512), 512)
        load = pltpu.make_async_copy(block_hbm, block, sem)
        load.start()
        load.wait()
        turned[0] = block[0].astype(F32).T.astype(BF16)
        turned[1] = (-block[1].astype(F32).T).astype(BF16)
        store = pltpu.make_async_copy(turned, out_hbm.at[:, :, lanes], sem)
        store.start()
        store.wait()


def last_pairs(place, block, visibility):
    return pl.pallas_call(
        last_kernel,
        out_shape=jax.ShapeDtypeStruct((2, 512, 2048), BF16),
        in_specs=[SMEM, ANY, ANY],
        out_specs=ANY,
        scratch_shapes=[pltpu.VMEM((2, 512, 512), BF16)] * 2 + [pltpu.SemaphoreType.DMA],
        input_output_aliases={2: 0},
        compiler_params=GRANT,
        cost_estimate=BRIEF,
        name="last_pairs",
    )(place, block, visibility)


def beam_kernel(at_ref, mask_ref, local_ref, near_ref, far_ref, end_ref, section_a, section_b, out_ref, weights):
    step, band = pl.program_id(0), at_ref[1]
    low = band < 2

    @pl.when(step == 0)
    def _():
        mask = mask_ref[...].astype(F32).astype(BF16)
        pieces = (
            (band, local_ref),
            (jnp.where(low, 2, 1), near_ref),
            (jnp.where(low, 3, 0), far_ref),
        )
        for group, piece_ref in pieces:
            lanes = pl.ds(pl.multiple_of(group * 512, 512), 512)
            wide = spread(mask, group)
            for part in range(2):
                weights[part * 256 : (part + 1) * 256, lanes] = piece_ref[part] * wide
        group = jnp.where(low, 1 - band, 5 - band)
        lanes = pl.ds(pl.multiple_of(group * 512, 512), 512)
        wide = spread(mask, group)
        inner = (band == 1) | (band == 2)
        for part in range(2):
            given = jnp.where(inner, end_ref[:, part * 512 : (part + 1) * 512] * wide, jnp.zeros((512,), BF16))
            weights[part * 256 : (part + 1) * 256, lanes] = given

    def form(section_ref):
        total = jnp.dot(weights[...], section_ref[...], preferred_element_type=F32)
        out_ref[:, :256] = total[:256, :256] - total[256:, 256:]
        out_ref[:, 256:] = total[:256, 256:] + total[256:, :256]

    pl.when(step < 2)(lambda: form(section_a))
    pl.when(step >= 2)(lambda: form(section_b))


def beams(place, mask, local, others, sections):
    return pl.pallas_call(
        beam_kernel,
        out_shape=jax.ShapeDtypeStruct((256, 2048), F32),
        grid_spec=pltpu.PrefetchScalarGridSpec(
            num_scalar_prefetch=1,
            grid=(4,),
            in_specs=[
                pl.BlockSpec((256, 64), lambda i, at: (at[1], 0)),
                pl.BlockSpec((2, 256, 512), lambda i, at: (0, at[1], 0)),
            ]
            + [pl.BlockSpec((2, 256, 512), lambda i, at: (0, 0, 0))] * 2
            + [
                pl.BlockSpec((256, 1024), lambda i, at: (0, 0)),
                pl.BlockSpec((2048, 512), lambda i, at: (0, jnp.minimum(i, 1))),
                pl.BlockSpec((2048, 512), lambda i, at: (0, jnp.maximum(i - 2, 0))),
            ],
            out_specs=pl.BlockSpec((256, 512), lambda i, at: (0, i)),
            scratch_shapes=[pltpu.VMEM((512, 2048), BF16)],
        ),
        compiler_params=GRANT,
        cost_estimate=BRIEF,
        name="beams",
    )(place, mask, local, *others, *sections)


def finish_kernel(at_ref, formed_ref, share_a, share_b, *refs):
    out_ref, turned = refs[-2:]
    is_outer = (at_ref[1] == 0) | (at_ref[1] == 3)
    for spectrum in range(4):
        share_ref = (share_a, share_b)[spectrum // 2]
        for part in range(2):
            at = spectrum * 512 + part * 256
            total = formed_ref[:, at : at + 256]
            at = at % 1024
            total = total + jnp.where(is_outer, share_ref[:, at : at + 256].astype(F32), 0.0)
            for lane in range(2):
                turned[lane, pl.ds(part * 4 + spectrum, 256, stride=8), :] = total[:, lane * 128 : (lane + 1) * 128]
    for lane in range(2):
        out_ref[:, :, lane * 128 : (lane + 1) * 128] = turned[lane].reshape(512, 4, 128).astype(BF16)


def finish(place, formed, shares, *after):
    return pl.pallas_call(
        finish_kernel,
        out_shape=jax.ShapeDtypeStruct((512, 4, 256), BF16),
        in_specs=[SMEM] + [VMEM] * 3 + [ANY] * len(after),
        out_specs=VMEM,
        scratch_shapes=[pltpu.VMEM((2, 2048, 128), F32)],
        compiler_params=GRANT,
        cost_estimate=BRIEF,
        name="finish",
    )(place, formed, *shares, *after)


def by_band(band, values):
    first, second, third, fourth = values
    return jnp.where(band < 2, jnp.where(band == 0, first, second), jnp.where(band == 2, third, fourth))


def shards(voltages, filter_taps, feed_gains, beam_weights, beam_mask, band_order):
    feed, band = lax.axis_index("feed"), lax.axis_index("band")
    half = lax.shift_right_logical(feed, 1) & 1
    low = band < 2
    everyone = (0, 1, 2, 3)
    place = jnp.stack([half, band])

    gains = feed_gains.reshape(2, 16, 2, 16, 256)
    sent_gain = lax.dynamic_index_in_dim(gains, 1 - half, 2, keepdims=False)
    entry_gains = (
        lax.ppermute(sent_gain, BOTH, hop(-3, (3,)) + hop(3, (0,))),
        lax.ppermute(sent_gain, BOTH, hop(-2, (2,)) + hop(2, (1,))),
    )
    own_weights = beam_weights[:, 0]
    from_near, from_far, from_end = hop(1, (1,)) + hop(-1, (2,)), hop(2, (0,)) + hop(-2, (3,)), hop(1, (0,)) + hop(-1, (3,))
    away = lax.dynamic_slice_in_dim(own_weights, jnp.where(low, 768, 0), 256, 1)
    near_outer = lax.ppermute(away, BOTH, from_near)
    far_outer = lax.ppermute(away, BOTH, from_far)

    spectra = channelize(voltages, filter_taps, band_order)
    got = lax.all_to_all(spectra, "feed", 0, 0, axis_index_groups=PLANE_GROUPS, tiled=True)
    got, near_outer, *entry_gains = lax.optimization_barrier((got, near_outer) + entry_gains)
    entry_gains[1], far_outer = lax.optimization_barrier((entry_gains[1], far_outer))
    ups, downs = [], []
    for section in range(2):
        up, down = ([part] for part in calibrate(section, place, got, gains))
        for step, senders in enumerate((everyone, everyone, (0, 1, 2), (1, 2))):
            up.append(lax.ppermute(up[-1], BOTH, hop(1, senders)))
            down.append(lax.ppermute(down[-1], BOTH, hop(-1, tuple(3 - p for p in senders))))
            if step < 2:
                up[-1] = enter(band == 0, up[-1], entry_gains[step])
                down[-1] = enter(band == 3, down[-1], entry_gains[step])
        ups.append(up)
        downs.append(down)

    average = 1.0 / 1024
    inward = hop(-1, (1,)) + hop(1, (2,))
    shares = []
    for up, down in zip(ups, downs):
        shares.append(outer_share(not shares, place, beam_mask, near_outer, far_outer, own_weights, up, down))
        if len(shares) == 1:
            block = edge(average, place, ups, downs, shares[0])
    shares[1], _ = lax.optimization_barrier((shares[1], block))
    received = lax.ppermute(block, BOTH, inward)
    shares = [
        lax.ppermute(shares[0], BOTH, inward + from_end),
        lax.ppermute(shares[1], BOTH, inward),
    ]

    away = lax.dynamic_slice_in_dim(own_weights, jnp.where(low, 512, 256), 256, 1)
    away, *_ = lax.optimization_barrier((away, block, shares[0]))
    near = lax.ppermute(away, BOTH, from_near)
    far = lax.ppermute(away, BOTH, from_far)

    visibility, sections = pairs(average, place, ups, downs, block, shares[0])
    visibility = last_pairs(place, received, visibility)
    formed = finish(place, beams(place, beam_mask, own_weights, (near, far, shares[0]), sections), shares, visibility)
    return (visibility[:, None], formed.reshape(1, 256, 2, 4, 256))


def solution(mesh):
    return jax.shard_map(
        shards,
        mesh=mesh,
        in_specs=(
            P(None, ("band", "feed"), None),
            P(),
            P(None, "feed", "band", None),
            P(None, "feed", None, "band"),
            P(),
            P(),
        ),
        out_specs=(P(None, "feed", "band", None), P("feed", "band", None, None, None)),
        check_vma=False,
    )
```
